256 devices in a mesh: member: 16 (over y, x), tile: 16 (over z, core).
Axes of the slice: x: 4, y: 4, z: 8, core: 2. Of those that a mesh axis runs over, the one named last changes fastest.
Arguments:
- ensemble_array: bfloat16 [64, 73, 96, 360], P('member', None, 'tile'), may hold values from -60 to 60
- lifting_matrix: bfloat16 [73, 256], replicated, may hold values from -0.75 to 0.75
- spectral_damping_factor: float32 [256, 96], replicated, may hold values from 0.1 to 1.9
- first_layer_matrix: bfloat16 [256, 512], replicated, may hold values from -0.375 to 0.375
- second_layer_matrix: bfloat16 [512, 256], replicated, may hold values from -0.25 to 0.25
- readout_matrix: bfloat16 [256, 73], replicated, may hold values from -0.375 to 0.375
- obs_count: int32 [256], P(('tile', 'member')), may hold values from 1 to 128, as said below
- obs_cell: int32 [256, 128], P(('tile', 'member')), may hold values from 0 to 134
- obs_op: float32 [256, 128, 73], P(('tile', 'member')), may hold values from -0.75 to 0.75
- obs_value: float32 [256, 128], P(('tile', 'member')), may hold values from -12 to 12
- obs_error: float32 [256, 128], P(('tile', 'member')), may hold values from 2 to 32
Outputs:
- analysis: bfloat16 [73, 34560, 64], P(None, ('tile', 'member'))
The draws below stay inside these ranges and needn't reach their ends.
Inputs may be any that keep to these rules, and one draw needn't show every extreme that they name: Observation slots i < obs_count of a tile are live, the rest ignored; some tile has all 128 live.
All inputs are finite; a program needn't handle non-finite values.
Results may differ from the reference program's by a relative error of at most 0.017.
Values may be sent and summed in bfloat16 or wider, within the bound.
A program may use at most 128 MiB of HBM per device.

```python
import math
import jax
import jax.numpy as jnp
from jax import lax

PHYSICAL_VARS = 73
EMB = 256
HID = 512
NLON = 360
MMAX = 96
OBS_MAX = 128
NS_ITERS = 24
ENSEMBLE_SIZE = 64
NLAT = 96
PATCH_POINTS = 135
NCELL = 34560
TILES = 256
N_MEMBER = 16
N_TILE = 16
DEVICES = 256


def draw_obs_count(key, part):
    key = jax.random.fold_in(key, 11)
    first, second = jax.random.split(key)
    counts = jax.random.randint(first, (DEVICES,), 1, OBS_MAX + 1)
    target = jax.random.randint(second, (), 0, DEVICES)
    spots = jnp.arange(DEVICES, dtype=jnp.int32)
    return jnp.where(spots == target, OBS_MAX, counts).astype(jnp.int32)


def member_field(key, lowest, highest, common, noise):
    scale_key, pick_key = jax.random.split(key)
    levels = jax.random.uniform(scale_key, (ENSEMBLE_SIZE,), jnp.float32, math.log(lowest), math.log(highest))
    picked = jax.random.randint(pick_key, (), 0, ENSEMBLE_SIZE)
    levels = jnp.where(jnp.arange(ENSEMBLE_SIZE, dtype=jnp.int32) == picked, math.log(highest), levels)
    member_scale = jnp.exp(levels)
    return common[None, :, :, :] + member_scale[:, None, None, None] * noise


def draw_ensemble_array(key, part):
    key = jax.random.fold_in(key, 23)
    scale_key, common_key, noise_key = jax.random.split(key, 3)
    shape = (ENSEMBLE_SIZE, PHYSICAL_VARS, NLAT, NLON)
    common = jnp.clip(jax.random.normal(common_key, shape[1:], jnp.float32), -4.0, 4.0)
    noise = jnp.clip(jax.random.normal(noise_key, shape, jnp.float32), -5.0, 5.0)
    values = member_field(scale_key, 0.03, 10.0, common, noise)
    return values.astype(jnp.bfloat16)


def with_ends(drawn, key, least, high):
    longest = drawn.shape.index(max(drawn.shape))
    spots = []
    for shift in (0, 1):
        where = [jax.random.randint(jax.random.fold_in(key, axis), (), 0, length) for axis, length in enumerate(drawn.shape)]
        where[longest] = (where[longest] + shift) % drawn.shape[longest]
        spots.append(tuple(where))
    return drawn.at[spots[0]].set(least).at[spots[1]].set(high)


def block_scale(rng, dims, shards, smallest, top_value):
    factor_of, own = 1.0, jax.random.fold_in(rng, 6)
    for axis_at, parts in shards:
        steps = jnp.exp(jax.random.uniform(jax.random.fold_in(own, axis_at), (parts,), jnp.float32, smallest / len(shards), top_value / len(shards)))
        factor_of = factor_of * jnp.repeat(steps, dims[axis_at] // parts).reshape([-1 if axis == axis_at else 1 for axis in range(len(dims))])
    return factor_of


def normal_values(key, shape, width, limit, pieces=(), held_as=jnp.bfloat16):
    level = block_scale(key, shape, pieces, -0.22, 0.18) if pieces else 1.0
    entries = jax.random.normal(key, shape, jnp.float32) * width * level
    return jnp.minimum(jnp.maximum(entries, -limit), limit).astype(held_as)


def setup_inputs(seed: int = 0) -> dict:
    seeds = jax.random.split(jax.random.key(seed), 12)
    ensemble_array = draw_ensemble_array(jax.random.fold_in(seeds[11], 71), 0)
    lifting_matrix = normal_values(seeds[1], (PHYSICAL_VARS, EMB), PHYSICAL_VARS ** -0.5, 0.75)
    spectral_damping_factor = jnp.clip(1.0 + 0.18 * jax.random.normal(seeds[2], (EMB, NLAT), jnp.float32), 0.1, 1.9)
    first_layer_matrix = normal_values(seeds[3], (EMB, HID), EMB ** -0.5, 0.375)
    second_layer_matrix = normal_values(seeds[4], (HID, EMB), HID ** -0.5, 0.25)
    readout_matrix = normal_values(seeds[5], (EMB, PHYSICAL_VARS), EMB ** -0.5, 0.375)
    obs_count = draw_obs_count(jax.random.fold_in(seeds[11], 71), 0)
    obs_cell = with_ends(jax.random.randint(seeds[7], (TILES, OBS_MAX), 0, PATCH_POINTS), jax.random.fold_in(seeds[7], 1), 0, PATCH_POINTS - 1).astype(jnp.int32)
    obs_op = normal_values(seeds[8], (TILES, OBS_MAX, PHYSICAL_VARS), PHYSICAL_VARS ** -0.5, 0.75, ((0, 256),), jnp.float32)
    obs_value = normal_values(seeds[9], (TILES, OBS_MAX), 2.0, 12.0, ((0, 256),), jnp.float32)
    obs_error = jnp.clip(jnp.exp(math.log(32.0) - 2.7725887 * jax.random.uniform(seeds[10], (TILES, OBS_MAX), jnp.float32) ** block_scale(seeds[10], (TILES, OBS_MAX), ((0, 256),), -0.2, 0.2)), 2.0, 32.0)
    return dict(ensemble_array=ensemble_array, lifting_matrix=lifting_matrix, spectral_damping_factor=spectral_damping_factor, first_layer_matrix=first_layer_matrix, second_layer_matrix=second_layer_matrix, readout_matrix=readout_matrix, obs_count=obs_count, obs_cell=obs_cell, obs_op=obs_op, obs_value=obs_value, obs_error=obs_error)


def lon_tables(nlon, mmax):
    lon = jnp.arange(nlon, dtype=jnp.float32)
    wave = jnp.arange(mmax, dtype=jnp.float32)
    phase = jnp.mod(lon[:, None] * wave[None, :], float(nlon))
    angle = 2.0 * math.pi * phase / nlon
    forward = jnp.concatenate([jnp.cos(angle), -jnp.sin(angle)], axis=1)
    factor = jnp.where(wave == 0.0, 1.0, 2.0).astype(jnp.float32) / nlon
    inverse = jnp.concatenate([jnp.cos(angle) * factor, -jnp.sin(angle) * factor], axis=1).T
    return (forward.astype(jnp.bfloat16), inverse.astype(jnp.bfloat16))

def lat_tables(nlat):
    row = jnp.arange(nlat, dtype=jnp.float32)
    phase = jnp.mod((2.0 * row[:, None] + 1.0) * row[None, :], float(4 * nlat))
    basis = jnp.cos(math.pi * phase / (2.0 * nlat))
    factor = jnp.where(row == 0.0, 1.0, 2.0).astype(jnp.float32) / nlat
    forward = (basis * factor[None, :]).T
    return (forward.astype(jnp.bfloat16), basis.astype(jnp.bfloat16))

def propagate_model(prior_values, lifting_matrix, spectral_damping_factor, first_layer_matrix, second_layer_matrix, readout_matrix):
    predicted_values = jnp.float32
    reduced_precision_source = jnp.bfloat16
    azimuthal_forward, azimuthal_inverse = lon_tables(NLON, MMAX)
    meridional_forward, meridional_inverse = lat_tables(NLAT)
    latent_activation = jnp.einsum('lgh,lt->tgh', prior_values.astype(predicted_values), lifting_matrix.astype(predicted_values)).astype(reduced_precision_source)
    transformed_coeffs = jnp.einsum('cmv,vn->cmn', latent_activation.astype(predicted_values), azimuthal_forward.astype(predicted_values)).astype(reduced_precision_source)
    harmonic_values = jnp.einsum('un,inj->iuj', meridional_forward.astype(predicted_values), transformed_coeffs.astype(predicted_values))
    harmonic_amplitude = (harmonic_values * spectral_damping_factor[:, :, None]).astype(reduced_precision_source)
    synthesis_result = jnp.einsum('sd,fdc->fsc', meridional_inverse.astype(predicted_values), harmonic_amplitude.astype(predicted_values)).astype(reduced_precision_source)
    physical_space_values = jnp.einsum('yvo,oh->yvh', synthesis_result.astype(predicted_values), azimuthal_inverse.astype(predicted_values)).astype(reduced_precision_source)
    blended_features = (latent_activation.astype(predicted_values) + physical_space_values.astype(predicted_values)).astype(reduced_precision_source)
    nested_body = jax.nn.gelu(jnp.einsum('dcv,dx->xcv', blended_features.astype(predicted_values), first_layer_matrix.astype(predicted_values))).astype(reduced_precision_source)
    enclosing_body = (blended_features.astype(predicted_values) + jnp.einsum('gwu,gx->xwu', nested_body.astype(predicted_values), second_layer_matrix.astype(predicted_values))).astype(reduced_precision_source)
    return (prior_values.astype(predicted_values) + jnp.einsum('jrk,jw->wrk', enclosing_body.astype(predicted_values), readout_matrix.astype(predicted_values))).astype(reduced_precision_source)

def tile_terms(patch_index, count, mesh_points, obs_op, value, error):
    predicted_values = jnp.float32
    latent_dimension = patch_index.shape[1]
    selection_matrix = (mesh_points[:, None] == jnp.arange(latent_dimension, dtype=jnp.int32)[None, :]).astype(predicted_values)
    selected_values = jnp.einsum('zv,rvg->zrg', selection_matrix, patch_index.astype(predicted_values))
    counterpart = jnp.einsum('jc,jcn->jn', obs_op, selected_values, precision=lax.Precision.HIGHEST)
    center = lax.optimization_barrier(jnp.mean(counterpart, axis=1))
    spread = counterpart - center[:, None]
    live = jnp.arange(obs_op.shape[0], dtype=jnp.int32) < count
    weight = jnp.where(live, 1.0 / error, jnp.zeros_like(error))
    gram = jnp.dot((spread * weight[:, None]).T, spread, precision=lax.Precision.HIGHEST)
    innov = jnp.dot(weight * (value - center), spread, precision=lax.Precision.HIGHEST)
    return (gram, innov)

def transform(gram, innov, ensemble_vectors):
    eye = jnp.eye(ensemble_vectors, dtype=jnp.float32)
    system = eye + gram / (ensemble_vectors - 1.0)
    lower = jnp.linalg.cholesky(system)
    mean_weight = jax.scipy.linalg.cho_solve((lower, True), innov) / (ensemble_vectors - 1.0)
    scale = jnp.sqrt(jnp.sum(system * system))

    def newton(step, carry):
        upper, root = carry
        shift = 1.5 * eye - 0.5 * jnp.dot(root, upper, precision=lax.Precision.HIGHEST)
        return (jnp.dot(upper, shift, precision=lax.Precision.HIGHEST), jnp.dot(shift, root, precision=lax.Precision.HIGHEST))
    upper, root = lax.fori_loop(0, NS_ITERS, newton, (system / scale, eye))
    return root / jnp.sqrt(scale) + mean_weight[:, None]

def update(patch_index, mix):
    base = patch_index.astype(jnp.float32)
    center = lax.optimization_barrier(jnp.mean(base, axis=2, keepdims=True))
    moved = jnp.einsum('ckf,fn->ckn', base - center, mix, precision=lax.Precision.HIGHEST)
    return (center + moved).astype(jnp.bfloat16)

def reference(ensemble_array, lifting_matrix, spectral_damping_factor, first_layer_matrix, second_layer_matrix, readout_matrix, obs_count, obs_cell, obs_op, obs_value, obs_error):
    prior_ensemble = lax.map(lambda prior_values: propagate_model(prior_values, lifting_matrix, spectral_damping_factor, first_layer_matrix, second_layer_matrix, readout_matrix), ensemble_array)
    update_patches = prior_ensemble.reshape(ENSEMBLE_SIZE, PHYSICAL_VARS, N_TILE, N_MEMBER, PATCH_POINTS).transpose(2, 3, 1, 4, 0).reshape(DEVICES, PHYSICAL_VARS, PATCH_POINTS, ENSEMBLE_SIZE)

    def stats(items):
        return tile_terms(*items)
    grams, innovs = lax.map(stats, (update_patches, obs_count, obs_cell, obs_op, obs_value, obs_error))
    mix = transform(lax.optimization_barrier(jnp.sum(grams, axis=0)), lax.optimization_barrier(jnp.sum(innovs, axis=0)), ENSEMBLE_SIZE)
    analysed = lax.map(lambda patch_index: update(patch_index, mix), update_patches)
    return analysed.transpose(1, 0, 2, 3).reshape(PHYSICAL_VARS, NCELL, ENSEMBLE_SIZE)
```

```python
import functools
import math

import jax
import jax.numpy as jnp
import numpy as np
from jax import lax
from jax.experimental import pallas as pl
from jax.experimental.pallas import tpu as pltpu
from jax.sharding import PartitionSpec as P

MMAX = 96
NS_ITERS = 24
BF = jnp.bfloat16
F32 = jnp.float32
HI = lax.Precision.HIGHEST
MESH = pl.DeviceIdType.MESH


def lon_tables(nlon, mmax):
    lon = np.arange(nlon, dtype=np.float64)
    wave = np.arange(mmax, dtype=np.float64)
    phase = np.mod(lon[:, None] * wave[None, :], float(nlon))
    angle = 2.0 * math.pi * phase / nlon
    forward = np.concatenate([np.cos(angle), -np.sin(angle)], axis=1)
    factor = np.where(wave == 0.0, 1.0, 2.0) / nlon
    inverse = np.concatenate([np.cos(angle) * factor, -np.sin(angle) * factor], axis=1).T
    return (forward.astype(np.float32).astype(BF), inverse.astype(np.float32).astype(BF))


def lat_tables(nlat):
    row = np.arange(nlat, dtype=np.float64)
    phase = np.mod((2.0 * row[:, None] + 1.0) * row[None, :], float(4 * nlat))
    basis = np.cos(math.pi * phase / (2.0 * nlat))
    factor = np.where(row == 0.0, 1.0, 2.0) / nlat
    forward = (basis * factor[None, :]).T
    return (forward.astype(np.float32).astype(BF), basis.astype(np.float32).astype(BF))


def reduce_kernel(nm, nt, part_ref, out_ref, got, mid, midg, fin, ssem, rsem):
    m, t = lax.axis_index("member"), lax.axis_index("tile")
    bar = pltpu.get_barrier_semaphore()

    def tile_peer(i):
        return (m, lax.rem(t + i, nt))

    def member_peer(i):
        return (lax.rem(m + i, nm), t)

    for i in range(1, nt):
        pl.semaphore_signal(bar, inc=1, device_id=tile_peer(i), device_id_type=MESH)
    for i in range(1, nm):
        pl.semaphore_signal(bar, inc=1, device_id=member_peer(i), device_id_type=MESH)
    pl.semaphore_wait(bar, nt + nm - 2)

    def send(src, dst, phase, i, dev):
        return pltpu.make_async_remote_copy(
            src_ref=src, dst_ref=dst, send_sem=ssem.at[phase, i], recv_sem=rsem.at[phase, i],
            device_id=dev, device_id_type=MESH)

    one = []
    for i in range(1, nt):
        c = send(part_ref.at[lax.rem(t + i, nt)], got.at[i], 0, i, tile_peer(i))
        c.start()
        one.append(c)
    acc = part_ref[t]
    for c in one:
        c.wait_recv()
    for i in range(1, nt):
        acc = acc + got[i]
    mid[...] = acc
    two = []
    for i in range(1, nm):
        c = send(mid, midg.at[lax.rem(m, nm)], 1, i, member_peer(i))
        c.start()
        two.append(c)
    midg[m] = acc
    for c in two:
        c.wait_recv()
    tot = midg[0]
    for i in range(1, nm):
        tot = tot + midg[i]
    out_ref[t] = tot
    fin[...] = tot
    three = []
    for i in range(1, nt):
        c = send(fin, out_ref.at[t], 2, i, tile_peer(i))
        c.start()
        three.append(c)
    for c in three:
        c.wait_recv()
    for c in one + two + three:
        c.wait_send()


def all_sum(part, nm, nt):
    vm = pl.BlockSpec(memory_space=pltpu.VMEM)
    return pl.pallas_call(
        functools.partial(reduce_kernel, nm, nt),
        out_shape=jax.ShapeDtypeStruct(part.shape, F32),
        in_specs=[vm],
        out_specs=vm,
        scratch_shapes=[
            pltpu.VMEM((nt, 8, 128), F32),
            pltpu.VMEM((8, 128), F32),
            pltpu.VMEM((nm, 8, 128), F32),
            pltpu.VMEM((8, 128), F32),
            pltpu.SemaphoreType.DMA((3, 16)),
            pltpu.SemaphoreType.DMA((3, 16)),
        ],
        compiler_params=pltpu.CompilerParams(collective_id=0, has_side_effects=True),
        name="all_sum",
    )(part)


def mix_of(stats, n):
    rows = lax.broadcasted_iota(jnp.int32, (n, n), 0)
    cols = lax.broadcasted_iota(jnp.int32, (n, n), 1)
    eye = (rows == cols).astype(F32)
    rw = lax.broadcasted_iota(jnp.int32, (n, 128), 0)
    cw = lax.broadcasted_iota(jnp.int32, (n, 128), 1)
    wide = jnp.where(cw < n, stats / (n - 1.0) + (rw == cw).astype(F32), stats)
    system = wide[:, :n]
    scale = jnp.sqrt(jnp.sum(system * system))
    up, root = system / scale, eye
    done = 0
    for it in range(NS_ITERS):
        shift = 1.5 * eye - 0.5 * jnp.dot(root, up, precision=HI, preferred_element_type=F32)
        up = jnp.dot(up, shift, precision=HI, preferred_element_type=F32)
        root = jnp.dot(shift, root, precision=HI, preferred_element_type=F32)
        upto = min(n, -(-n * (it + 1) // NS_ITERS))
        for j in range(done, upto):
            r = wide[j:j + 1, :]
            r = r / wide[j:j + 1, j:j + 1]
            col = wide[:, j:j + 1] - (rw[:, :1] == j).astype(F32)
            wide = wide - col * r
        done = upto
    weight = wide[:, n:n + 1] / (n - 1.0)
    return root / jnp.sqrt(scale) + weight


def mix_kernel(stats_ref, mix_ref):
    mix_ref[...] = mix_of(stats_ref[...], mix_ref.shape[0])


def mix_call(stats, n):
    vm = pl.BlockSpec(memory_space=pltpu.VMEM)
    return pl.pallas_call(
        mix_kernel,
        out_shape=jax.ShapeDtypeStruct((n, n), F32),
        in_specs=[vm],
        out_specs=vm,
        name="mix",
    )(stats)


def tile_terms(patch, count, cells, obs_op, value, error):
    ncell = patch.shape[1]
    sel = (cells[:, None] == jnp.arange(ncell, dtype=jnp.int32)[None, :]).astype(BF)
    picked = jnp.einsum("zv,rvg->zrg", sel, patch, preferred_element_type=F32)
    counterpart = jnp.einsum("jc,jcn->jn", obs_op, picked, precision=HI)
    center = jnp.mean(counterpart, axis=1)
    spread = counterpart - center[:, None]
    live = jnp.arange(obs_op.shape[0], dtype=jnp.int32) < count
    weight = jnp.where(live, 1.0 / error, jnp.zeros_like(error))
    both = jnp.concatenate([spread, (value - center)[:, None]], axis=1)
    return jnp.dot((spread * weight[:, None]).T, both, precision=HI)


def update(patch, mix):
    base = patch.astype(F32)
    center = jnp.mean(base, axis=2, keepdims=True)
    moved = jnp.einsum("ckf,fn->ckn", base - center, mix, precision=HI)
    return (center + moved).astype(BF)


def shards(x, lift, gain, w1, w2, readout, obs_count, obs_cell, obs_op, obs_value, obs_error):
    mem, nvar, rows, nlon = x.shape
    nt, nm = lax.axis_size("tile"), lax.axis_size("member")
    nlat = rows * nt
    emb = lift.shape[1]
    t = lax.axis_index("tile")
    lon_f, lon_i = (jnp.asarray(a) for a in lon_tables(nlon, MMAX))
    lat_f, lat_i = (jnp.asarray(a) for a in lat_tables(nlat))
    k = 2 * MMAX
    own = rows * nvar
    hatx = jnp.einsum("mcpq,qk->pcmk", x, lon_f, preferred_element_type=F32).astype(BF)
    hatx = jnp.pad(hatx.reshape(own, mem * k), ((0, 448 - own), (0, 0)))
    hats = lax.all_gather(hatx, "tile", axis=0, tiled=True)
    band = lax.dynamic_slice_in_dim(lat_i, t * rows, rows, 0).astype(F32)
    g = (band[:, None, :] * gain[None, :, :]).reshape(rows * emb, nlat)
    tr = jnp.dot(g, lat_f.astype(F32), precision=HI)
    w = tr.reshape(rows, emb, nt, rows, 1) * lift.T.astype(F32)[None, :, None, None, :]
    w = w.astype(BF).reshape(rows * emb, nt, own)
    w = jnp.pad(w, ((0, 0), (0, 0), (0, 448 - own))).reshape(rows * emb, nt * 448)
    back = jnp.dot(w, hats, preferred_element_type=F32).astype(BF).reshape(rows, emb, mem, k)
    spatial = jnp.einsum("pemk,kq->mepq", back, lon_i, preferred_element_type=F32).astype(BF)
    hid = jnp.einsum("mcpq,ce->mepq", x, lift, preferred_element_type=F32).astype(BF)
    mixed = (hid.astype(F32) + spatial.astype(F32)).astype(BF)
    inner = jax.nn.gelu(jnp.einsum("mepq,eh->mhpq", mixed, w1, preferred_element_type=F32)).astype(BF)
    outer = (mixed.astype(F32) + jnp.einsum("mhpq,he->mepq", inner, w2, preferred_element_type=F32)).astype(BF)
    lifted = jnp.einsum("mepq,ec->cpqm", outer, readout, preferred_element_type=F32)
    forecast = (jnp.transpose(x, (1, 2, 3, 0)).astype(F32) + lifted).astype(BF)
    ncell = rows * nlon // nm
    lines = forecast.reshape(nvar, nm, ncell, mem)
    patch = lax.all_to_all(lines, "member", split_axis=1, concat_axis=3, tiled=True)
    patch = patch.reshape(nvar, ncell, mem * nm)
    n = mem * nm
    part = tile_terms(patch, obs_count[0], obs_cell[0], obs_op[0], obs_value[0], obs_error[0])
    part = jnp.pad(part.reshape(nt, n // nt, n + 1), ((0, 0), (0, 8 - n // nt), (0, 127 - n)))
    stats = all_sum(part, nm, nt)[:, : n // nt].reshape(n, 128)
    return update(patch, mix_call(stats, n))


def solution(mesh):
    placed = (
        P("member", None, "tile", None),
        P(), P(), P(), P(), P(),
        P(("tile", "member")),
        P(("tile", "member"), None),
        P(("tile", "member"), None, None),
        P(("tile", "member"), None),
        P(("tile", "member"), None),
    )
    return jax.shard_map(
        shards, mesh=mesh, in_specs=placed, out_specs=P(None, ("tile", "member"), None), check_vma=False)
```

```python
import functools
import math

import jax
import jax.numpy as jnp
import numpy as np
from jax import lax
from jax.experimental import pallas as pl
from jax.experimental.pallas import tpu as pltpu
from jax.sharding import PartitionSpec as P

MMAX = 96
NS_ITERS = 24
BF = jnp.bfloat16
F32 = jnp.float32
HI = lax.Precision.HIGHEST
MESH = pl.DeviceIdType.MESH


def lon_tables(nlon, mmax):
    lon = np.arange(nlon, dtype=np.float64)
    wave = np.arange(mmax, dtype=np.float64)
    phase = np.mod(lon[:, None] * wave[None, :], float(nlon))
    angle = 2.0 * math.pi * phase / nlon
    forward = np.concatenate([np.cos(angle), -np.sin(angle)], axis=1)
    factor = np.where(wave == 0.0, 1.0, 2.0) / nlon
    inverse = np.concatenate([np.cos(angle) * factor, -np.sin(angle) * factor], axis=1).T
    return (forward.astype(np.float32).astype(BF), inverse.astype(np.float32).astype(BF))


def lat_tables(nlat):
    row = np.arange(nlat, dtype=np.float64)
    phase = np.mod((2.0 * row[:, None] + 1.0) * row[None, :], float(4 * nlat))
    basis = np.cos(math.pi * phase / (2.0 * nlat))
    factor = np.where(row == 0.0, 1.0, 2.0) / nlat
    forward = (basis * factor[None, :]).T
    return (forward.astype(np.float32).astype(BF), basis.astype(np.float32).astype(BF))


VARS, CPAD = 73, 80
ROWS, NLON, NLAT = 6, 360, 96
KCOL = 2 * MMAX
CHUNK = 448
CELLS = 2304
EMB, HID = 256, 512
NZ = 8


def chunk_index():
    lat = np.full(CHUNK, -1)
    chan = np.full(CHUNK, -1)
    for p in range(ROWS):
        lat[64 * p:64 * p + 64], chan[64 * p:64 * p + 64] = p, np.arange(64)
        at = 384 + 9 * p
        lat[at:at + 9], chan[at:at + 9] = p, np.arange(64, 73)
    return lat, chan


def window(p):
    start = 128 * (360 * p // 128)
    return start, min(512, CELLS - start)


def kernel_tables():
    lon_f, lon_i = (np.asarray(a).astype(np.float32) for a in lon_tables(NLON, MMAX))
    lat_f, lat_i = (np.asarray(a).astype(np.float32) for a in lat_tables(NLAT))
    fw = np.zeros((ROWS, 512, 256), np.float32)
    for p in range(ROWS):
        at = 360 * p - window(p)[0]
        fw[p, at:at + 360, :KCOL] = lon_f
    iv = np.zeros((9, 2, 256, 256), np.float32)
    for n in range(9):
        low = min(256 * n // 360, 4)
        for s in range(2):
            for col in range(256):
                q = 256 * n + col - 360 * (low + s)
                if 0 <= q < 360:
                    iv[n, s, :KCOL, col] = lon_i[:, q]
    lat, chan = chunk_index()
    lf = np.zeros((16, 256, CHUNK), np.float32)
    for t in range(16):
        cols = lat_f[:, 6 * t + np.maximum(lat, 0)] * (lat >= 0)
        lf[t, :NLAT], lf[t, 128:128 + NLAT] = cols, cols
    lf = lf.reshape(NZ, 2, 256, CHUNK).transpose(0, 2, 1, 3).reshape(NZ, 256, 2 * CHUNK)
    li = np.zeros((NLAT, 128), np.float32)
    li[:, :NLAT] = lat_i
    return fw.astype(BF), iv.reshape(9, 512, 256).astype(BF), lf.astype(BF), li


def dot(a, b):
    return jnp.dot(a, b, preferred_element_type=F32)


def forecast_kernel(nm, x_ref, fw_ref, iv_ref, lf_ref, li_ref, gain_ref, lx_ref, lt_ref, w1_ref, w2_ref, ro_ref,
                    count_ref, cell_ref, op_ref, val_ref, err_ref,
                    field_ref, stats_ref,
                    spec, wmat, acc, bk, fs, cp, lx2, part, got, mid, midg, fin,
                    ag_s, ag_r, ax_s, ax_r, rs_s, rs_r):
    m, t = lax.axis_index("member"), lax.axis_index("tile")
    nt = 2 * NZ
    z, core = t // 2, lax.rem(t, 2)

    def zat(d):
        return lax.rem(z + d + NZ, NZ)

    def member_peer(i):
        return (lax.rem(m + i, nm), t)

    def tile_peer(i):
        return (m, lax.rem(t + i, nt))

    right, left, sib = (m, zat(1) * 2 + core), (m, zat(-1) * 2 + core), (m, z * 2 + 1 - core)
    bar = pltpu.get_barrier_semaphore()
    for i in range(1, nt):
        pl.semaphore_signal(bar, inc=1, device_id=tile_peer(i), device_id_type=MESH)
    for i in range(1, nm):
        pl.semaphore_signal(bar, inc=1, device_id=member_peer(i), device_id_type=MESH)

    low64 = lax.broadcasted_iota(jnp.int32, (CPAD, 128), 1) < 64

    def spectra(q):
        tails = []
        for p in range(ROWS):
            at, wide = window(p)
            v0 = dot(x_ref[2 * q, :, at:at + wide], fw_ref[p, :wide])
            v1 = dot(x_ref[2 * q + 1, :, at:at + wide], fw_ref[p, :wide])
            mixed = jnp.where(low64, v0[:, 128:], pltpu.roll(v1[:, 128:], 64, 1))
            v = jnp.concatenate([v0[:, :128], mixed, v1[:, :128]], axis=1)
            spec[q, t, 64 * p:64 * p + 64] = v[:64].astype(BF)
            tails.append(v[64:VARS])
        tails.append(jnp.zeros((10, 384), F32))
        spec[q, t, 384:CHUNK] = jnp.concatenate(tails, axis=0).astype(BF)

    sent = []

    def half(h):
        return pl.ds(0, CHUNK) if h is None else pl.ds(h * (CHUNK // 2), CHUNK // 2)

    def copy(q, dz, other, h, sem, dev):
        ref = spec.at[q, zat(dz) * 2 + (1 - core if other else core), half(h)]
        return pltpu.make_async_remote_copy(
            src_ref=ref, dst_ref=ref, send_sem=ag_s.at[q, sem], recv_sem=ag_r.at[q, sem],
            device_id=dev, device_id_type=MESH)

    def go(c):
        c.start()
        sent.append(c)

    def own(q):
        for h in range(2):
            go(copy(q, 0, False, h, h, right))
            go(copy(q, 0, False, h, 7 + h, left))
        go(copy(q, 0, False, None, 14, sib))

    def step(q, d, h):
        if d < 4 or h == 0:
            copy(q, -d, False, h, 2 * (d - 1) + h, right).wait_recv()
            if d < 3 or (d == 3 and h == 0):
                go(copy(q, -d, False, h, 2 * d + h, right))
        if d < 4 or h == 1:
            copy(q, d, False, h, 7 + (2 * (d - 1) + h if d < 4 else 6), left).wait_recv()
            if d < 3 or (d == 3 and h == 1):
                go(copy(q, d, False, h, 7 + (2 * d + h if d < 3 else 6), left))
        if d == 4:
            go(copy(q, 4, False, h, 21 + h, sib))
        elif h == 1:
            go(copy(q, -d, False, None, 14 + d, sib))
            go(copy(q, d, False, None, 17 + d, sib))

    def from_sib(q, d):
        if d == 0:
            copy(q, 0, True, None, 14, sib).wait_recv()
        elif d == 4:
            copy(q, 4, True, 0, 21, sib).wait_recv()
            copy(q, 4, True, 1, 22, sib).wait_recv()
        elif d < 0:
            copy(q, d, True, None, 14 - d, sib).wait_recv()
        else:
            copy(q, d, True, None, 17 + d, sib).wait_recv()

    def weights(d):
        zz = zat(d)

        @pl.loop(0, ROWS)
        def _(p):
            g = gain_ref[...] * li_ref[pl.ds(ROWS * t + p, 1), :]
            hi = g.astype(BF)
            lo = (g - hi.astype(F32)).astype(BF)
            w = dot(jnp.concatenate([hi, lo], axis=1), lf_ref[zz])
            wmat[zz, pl.ds(pl.multiple_of(p * EMB, EMB), EMB), :] = (w * lx2[...]).astype(BF)

    def apply(q, d):
        zz = zat(d)
        g = spec[q, pl.ds(zz * 2, 2)].reshape(2 * CHUNK, 384)

        @pl.loop(0, 3)
        def _(b):
            rows = pl.ds(pl.multiple_of(b * 512, 512), 512)
            v = dot(wmat[zz, rows, :], g)
            acc[q, rows, :] = v if d == 0 else acc[q, rows, :] + v

    c0 = math.sqrt(2.0 / math.pi)

    def member(e):
        q = e // 2

        @pl.loop(0, ROWS)
        def _(p):
            a = acc[q, pl.ds(pl.multiple_of(p * EMB, EMB), EMB), :]
            if e % 2:
                a = jnp.concatenate([a[:, 256:], pltpu.roll(a[:, 128:256], 64, 1)], axis=1)
            else:
                a = a[:, :256]
            bk[p] = a.astype(BF)

        @pl.loop(0, 9)
        def _(n):
            low = jnp.minimum(256 * n // 360, 4)
            lanes = pl.ds(pl.multiple_of(n * 256, 256), 256)
            x = x_ref[e, :, lanes]
            s = dot(jnp.concatenate([bk[low], bk[low + 1]], axis=1), iv_ref[n])
            mixed = (s + dot(lt_ref[...], x)).astype(BF)
            u = dot(w1_ref[...], mixed)
            u = 0.5 * u * (1.0 + jnp.tanh(c0 * (u + 0.044715 * (u * u * u))))
            outer = (mixed.astype(F32) + dot(w2_ref[...], u.astype(BF))).astype(BF)
            fs[e, :, lanes] = (x.astype(F32) + dot(ro_ref[...], outer)).astype(BF)

        for i in range(1, nm):
            go(out_copy(e, i))
        field_ref[4 * m + e] = fs[e, :, pl.ds(pl.multiple_of(128 * m, 128), 256)]

    def out_copy(e, i):
        to = lax.rem(m + i, nm)
        return pltpu.make_async_remote_copy(
            src_ref=fs.at[e, :, pl.ds(pl.multiple_of(128 * to, 128), 256)], dst_ref=field_ref.at[4 * m + e],
            send_sem=ax_s.at[e, i], recv_sem=ax_r.at[e, i], device_id=(to, t), device_id_type=MESH)

    spectra(0)
    pl.semaphore_wait(bar, nt + nm - 2)
    own(0)
    spectra(1)
    lx2[...] = lx_ref[...].astype(F32)
    for d in (0, 1, -1):
        weights(d)
    step(0, 1, 0)
    weights(2)
    step(0, 1, 1)
    weights(-2)
    from_sib(0, 0)
    apply(0, 0)
    step(0, 2, 0)
    weights(3)
    from_sib(0, 1)
    apply(0, 1)
    step(0, 2, 1)
    weights(-3)
    from_sib(0, -1)
    apply(0, -1)
    own(1)
    step(0, 3, 0)
    weights(4)
    from_sib(0, 2)
    apply(0, 2)
    step(0, 3, 1)
    from_sib(0, -2)
    apply(0, -2)
    step(0, 4, 0)
    step(0, 4, 1)
    from_sib(1, 0)
    apply(1, 0)
    from_sib(0, 3)
    apply(0, 3)
    step(1, 1, 0)
    from_sib(0, -3)
    apply(0, -3)
    step(1, 1, 1)
    from_sib(0, 4)
    apply(0, 4)
    step(1, 2, 0)
    member(0)
    step(1, 2, 1)
    from_sib(1, 1)
    apply(1, 1)
    from_sib(1, -1)
    apply(1, -1)
    step(1, 3, 0)
    member(1)
    step(1, 3, 1)
    from_sib(1, 2)
    apply(1, 2)
    from_sib(1, -2)
    apply(1, -2)
    step(1, 4, 0)
    step(1, 4, 1)
    from_sib(1, 3)
    apply(1, 3)
    from_sib(1, -3)
    apply(1, -3)
    from_sib(1, 4)
    apply(1, 4)
    member(2)
    member(3)

    cells = cell_ref[...] + 7 * m
    pick = (lax.broadcasted_iota(jnp.int32, (256, 128), 0) == cells).astype(BF)
    ident = (lax.broadcasted_iota(jnp.int32, (CPAD, VARS), 0)
             == lax.broadcasted_iota(jnp.int32, (CPAD, VARS), 1)).astype(F32)
    nt_dims = (((1,), (1,)), ((), ()))
    op = lax.dot_general(ident, op_ref[...], nt_dims, precision=HI, preferred_element_type=F32)

    def counterparts(e, src):
        f = 4 * src + e
        v = dot(field_ref[f], pick) * op
        cp[pl.ds(f, 1), :] = jnp.sum(v, axis=0, keepdims=True)

    for e in range(4):
        for i in range(nm):
            if i:
                out_copy(e, i).wait_recv()
            counterparts(e, lax.rem(m - i + nm, nm))
    c = cp[...]
    n = c.shape[0]
    ybar = jnp.mean(c, axis=0, keepdims=True)
    spread = c - ybar
    live = lax.broadcasted_iota(jnp.int32, (1, 128), 1) < count_ref[...]
    weight = jnp.where(live, 1.0 / err_ref[...], 0.0)
    both = jnp.concatenate([spread, val_ref[...] - ybar, jnp.zeros((127 - n, 128), F32)], axis=0)
    gram = lax.dot_general(spread * weight, both, nt_dims, precision=HI, preferred_element_type=F32)
    per = n // nt
    for b in range(nt):
        part[b, :per] = gram[per * b:per * b + per]
        part[b, per:] = jnp.zeros((8 - per, 128), F32)

    def send(src, dst, phase, i, dev):
        cc = pltpu.make_async_remote_copy(
            src_ref=src, dst_ref=dst, send_sem=rs_s.at[phase, i], recv_sem=rs_r.at[phase, i],
            device_id=dev, device_id_type=MESH)
        go(cc)
        return cc

    one = [send(part.at[lax.rem(t + i, nt)], got.at[i], 0, i, tile_peer(i)) for i in range(1, nt)]
    tot = part[t]
    for cc in one:
        cc.wait_recv()
    for i in range(1, nt):
        tot = tot + got[i]
    mid[...] = tot
    two = [send(mid, midg.at[m], 1, i, member_peer(i)) for i in range(1, nm)]
    midg[m] = tot
    for cc in two:
        cc.wait_recv()
    tot = midg[0]
    for i in range(1, nm):
        tot = tot + midg[i]
    stats_ref[t] = tot
    fin[...] = tot
    three = [send(fin, stats_ref.at[t], 2, i, tile_peer(i)) for i in range(1, nt)]
    for cc in three:
        cc.wait_recv()
    for cc in sent:
        cc.wait_send()


def forecast_call(args, nm, nt, n):
    vm = pl.BlockSpec(memory_space=pltpu.VMEM)
    dma = pltpu.SemaphoreType.DMA
    return pl.pallas_call(
        functools.partial(forecast_kernel, nm),
        out_shape=[jax.ShapeDtypeStruct((n, CPAD, 256), BF), jax.ShapeDtypeStruct((nt, 8, 128), F32)],
        in_specs=[vm] * len(args),
        out_specs=[vm, vm],
        scratch_shapes=[
            pltpu.VMEM((2, nt, CHUNK, 384), BF),
            pltpu.VMEM((NZ, ROWS * EMB, 2 * CHUNK), BF),
            pltpu.VMEM((2, ROWS * EMB, 384), F32),
            pltpu.VMEM((ROWS, EMB, 256), BF),
            pltpu.VMEM((4, CPAD, CELLS), BF),
            pltpu.VMEM((n, 128), F32),
            pltpu.VMEM((EMB, 2 * CHUNK), F32),
            pltpu.VMEM((nt, 8, 128), F32),
            pltpu.VMEM((nt, 8, 128), F32),
            pltpu.VMEM((8, 128), F32),
            pltpu.VMEM((nm, 8, 128), F32),
            pltpu.VMEM((8, 128), F32),
            dma((2, 23)), dma((2, 23)), dma((4, 16)), dma((4, 16)), dma((3, 16)), dma((3, 16)),
        ],
        compiler_params=pltpu.CompilerParams(
            collective_id=0, has_side_effects=True, vmem_limit_bytes=62 * 2**20),
        name="forecast",
    )(*args)


def mix_of(stats, n):
    rows = lax.broadcasted_iota(jnp.int32, (n, n), 0)
    cols = lax.broadcasted_iota(jnp.int32, (n, n), 1)
    eye = (rows == cols).astype(F32)
    rw = lax.broadcasted_iota(jnp.int32, (n, 128), 0)
    cw = lax.broadcasted_iota(jnp.int32, (n, 128), 1)
    wide = jnp.where(cw < n, stats / (n - 1.0) + (rw == cw).astype(F32), stats)
    system = wide[:, :n]
    scale = jnp.sqrt(jnp.sum(system * system))
    up, root = system / scale, eye
    done = 0
    for it in range(NS_ITERS):
        shift = 1.5 * eye - 0.5 * jnp.dot(root, up, precision=HI, preferred_element_type=F32)
        up = jnp.dot(up, shift, precision=HI, preferred_element_type=F32)
        root = jnp.dot(shift, root, precision=HI, preferred_element_type=F32)
        upto = min(n, -(-n * (it + 1) // NS_ITERS))
        for j in range(done, upto):
            r = wide[j:j + 1, :]
            r = r / wide[j:j + 1, j:j + 1]
            col = wide[:, j:j + 1] - (rw[:, :1] == j).astype(F32)
            wide = wide - col * r
        done = upto
    weight = wide[:, n:n + 1] / (n - 1.0)
    return root / jnp.sqrt(scale) + weight


def mix_kernel(stats_ref, mix_ref):
    mix_ref[...] = mix_of(stats_ref[...], mix_ref.shape[0])


def mix_call(stats, n):
    vm = pl.BlockSpec(memory_space=pltpu.VMEM)
    return pl.pallas_call(
        mix_kernel,
        out_shape=jax.ShapeDtypeStruct((n, n), F32),
        in_specs=[vm],
        out_specs=vm,
        name="mix",
    )(stats)


def update(patch, mix):
    base = patch.astype(F32)
    center = jnp.mean(base, axis=2, keepdims=True)
    moved = jnp.einsum("ckf,fn->ckn", base - center, mix, precision=HI)
    return (center + moved).astype(BF)


def shards(x, lift, gain, w1, w2, readout, obs_count, obs_cell, obs_op, obs_value, obs_error):
    mem, nvar, rows, nlon = x.shape
    nt, nm = lax.axis_size("tile"), lax.axis_size("member")
    n = mem * nm
    ncell = rows * nlon // nm
    fw, iv, lf, li = (jnp.asarray(a) for a in kernel_tables())
    xk = jnp.pad(x.reshape(mem, nvar, rows * nlon), ((0, 0), (0, CPAD - nvar), (0, CELLS - rows * nlon)))
    lt = lift.T
    one = jnp.concatenate([jnp.tile(lt[:, :64], (1, ROWS)), jnp.tile(lt[:, 64:], (1, ROWS)), jnp.zeros((EMB, 10), BF)], axis=1)
    lx = jnp.concatenate([one, one], axis=1)
    ltp = jnp.pad(lt, ((0, 0), (0, CPAD - nvar)))
    ro = jnp.pad(readout.T, ((0, CPAD - nvar), (0, 0)))
    gp = jnp.pad(gain, ((0, 0), (0, 128 - gain.shape[1])))
    args = (xk, fw, iv, lf, li, gp, lx, ltp, w1.T, w2.T, ro,
            obs_count.reshape(1, 1), obs_cell, obs_op[0], obs_value, obs_error)
    field, stats = forecast_call(args, nm, nt, n)
    stats = stats[:, : n // nt].reshape(n, 128)
    mix = mix_call(stats, n)
    patch = lax.dynamic_slice(field, (0, 0, 7 * lax.axis_index("member")), (n, nvar, ncell))
    return update(jnp.transpose(patch, (1, 2, 0)), mix)


def solution(mesh):
    placed = (
        P("member", None, "tile", None),
        P(), P(), P(), P(), P(),
        P(("tile", "member")),
        P(("tile", "member"), None),
        P(("tile", "member"), None, None),
        P(("tile", "member"), None),
        P(("tile", "member"), None),
    )
    return jax.shard_map(
        shards, mesh=mesh, in_specs=placed, out_specs=P(None, ("tile", "member"), None), check_vma=False)
```

```python
import functools
import math

import jax
import jax.numpy as jnp
import numpy as np
from jax import lax
from jax.experimental import pallas as pl
from jax.experimental.pallas import tpu as pltpu
from jax.sharding import PartitionSpec as P

MMAX = 96
NS_ITERS = 24
BF = jnp.bfloat16
F32 = jnp.float32
HI = lax.Precision.HIGHEST
MESH = pl.DeviceIdType.MESH


def lon_tables(nlon, mmax):
    lon = np.arange(nlon, dtype=np.float64)
    wave = np.arange(mmax, dtype=np.float64)
    phase = np.mod(lon[:, None] * wave[None, :], float(nlon))
    angle = 2.0 * math.pi * phase / nlon
    forward = np.concatenate([np.cos(angle), -np.sin(angle)], axis=1)
    factor = np.where(wave == 0.0, 1.0, 2.0) / nlon
    inverse = np.concatenate([np.cos(angle) * factor, -np.sin(angle) * factor], axis=1).T
    return (forward.astype(np.float32).astype(BF), inverse.astype(np.float32).astype(BF))


def lat_tables(nlat):
    row = np.arange(nlat, dtype=np.float64)
    phase = np.mod((2.0 * row[:, None] + 1.0) * row[None, :], float(4 * nlat))
    basis = np.cos(math.pi * phase / (2.0 * nlat))
    factor = np.where(row == 0.0, 1.0, 2.0) / nlat
    forward = (basis * factor[None, :]).T
    return (forward.astype(np.float32).astype(BF), basis.astype(np.float32).astype(BF))


VARS, CPAD = 73, 80
ROWS, NLON, NLAT = 6, 360, 96
KCOL = 2 * MMAX
CHUNK = 448
CELLS = 2304
EMB, HID = 256, 512
NZ = 8
NCELL = 135


def chunk_index():
    lat = np.full(CHUNK, -1)
    chan = np.full(CHUNK, -1)
    for p in range(ROWS):
        lat[64 * p:64 * p + 64], chan[64 * p:64 * p + 64] = p, np.arange(64)
        at = 384 + 9 * p
        lat[at:at + 9], chan[at:at + 9] = p, np.arange(64, 73)
    return lat, chan


def window(p):
    start = 128 * (360 * p // 128)
    return start, min(512, CELLS - start)


def kernel_tables():
    lon_f, lon_i = (np.asarray(a).astype(np.float32) for a in lon_tables(NLON, MMAX))
    lat_f, lat_i = (np.asarray(a).astype(np.float32) for a in lat_tables(NLAT))
    fw = np.zeros((ROWS, 512, 256), np.float32)
    for p in range(ROWS):
        at = 360 * p - window(p)[0]
        fw[p, at:at + 360, :KCOL] = lon_f
    iv = np.zeros((9, 2, 256, 256), np.float32)
    for n in range(9):
        low = min(256 * n // 360, 4)
        for s in range(2):
            for col in range(256):
                q = 256 * n + col - 360 * (low + s)
                if 0 <= q < 360:
                    iv[n, s, :KCOL, col] = lon_i[:, q]
    lat, chan = chunk_index()
    lf = np.zeros((16, NLAT, CHUNK), np.float32)
    for t in range(16):
        lf[t] = lat_f[:, 6 * t + np.maximum(lat, 0)] * (lat >= 0)
    lf = lf.reshape(NZ, 2, NLAT, CHUNK).transpose(0, 2, 1, 3).reshape(NZ, NLAT, 2 * CHUNK)
    spread = (chan[None, :] == np.arange(VARS)[:, None]).astype(np.float32)
    spread = np.concatenate([spread, spread], axis=1)
    return fw.astype(BF), iv.reshape(9, 512, 256).astype(BF), lf.astype(BF), lat_i, spread.astype(BF)


def dot(a, b):
    return jnp.dot(a, b, preferred_element_type=F32)


def forecast_kernel(nm, x_ref, fw_ref, iv_ref, lf_ref, li_ref, sp_ref, gain_ref, lift_ref, w1_ref, w2_ref, ro_ref,
                    count_ref, cell_ref, op_ref, val_ref, err_ref,
                    ft_ref, stats_ref,
                    spec, wmat, acc, bk, fs, field_ref, cp, lx, lt, w1t, w2t, rot, gt, turn, stage, part, got, mid, midg, fin,
                    ag_s, ag_r, ax_s, ax_r, rs_s, rs_r):
    m, t = lax.axis_index("member"), lax.axis_index("tile")
    nt = 2 * NZ
    z, core = t // 2, lax.rem(t, 2)

    def zat(d):
        return lax.rem(z + d + NZ, NZ)

    def member_peer(i):
        return (lax.rem(m + i, nm), t)

    def tile_peer(i):
        return (m, lax.rem(t + i, nt))

    right, left, sib = (m, zat(1) * 2 + core), (m, zat(-1) * 2 + core), (m, z * 2 + 1 - core)
    bar = pltpu.get_barrier_semaphore()
    for i in range(1, nt):
        pl.semaphore_signal(bar, inc=1, device_id=tile_peer(i), device_id_type=MESH)
    for i in range(1, nm):
        pl.semaphore_signal(bar, inc=1, device_id=member_peer(i), device_id_type=MESH)

    low64 = lax.broadcasted_iota(jnp.int32, (CPAD, 128), 1) < 64
    low64e = lax.broadcasted_iota(jnp.int32, (EMB, 128), 1) < 64

    def half_turn(v):
        return pltpu.roll(v, 64, 1)

    def spectra(pieces):
        tails = {i: [] for i in pieces}
        for p in range(ROWS):
            at, wide = window(p)

            def both(e):
                v = dot(x_ref[e, :, at:at + wide], fw_ref[p, :wide])
                return v[:, :128], v[:, 128:]

            for i in pieces:
                if i == 0:
                    (a0, b0), (a1, _) = both(0), both(1)
                    v = [a0, jnp.where(low64, b0, half_turn(a1))]
                elif i == 1:
                    (a1, b1), (a2, _) = both(1), both(2)
                    v = [jnp.where(low64, half_turn(a1), half_turn(b1)), a2]
                else:
                    (_, b2), (a3, b3) = both(2), both(3)
                    a3 = half_turn(a3)
                    v = [jnp.where(low64, b2, a3), jnp.where(low64, a3, half_turn(b3))]
                v = jnp.concatenate(v, axis=1)
                spec[i, t, 64 * p:64 * p + 64] = v[:64].astype(BF)
                tails[i].append(v[64:VARS])
        for i in pieces:
            tails[i].append(jnp.zeros((10, 256), F32))
            spec[i, t, 384:CHUNK] = jnp.concatenate(tails[i], axis=0).astype(BF)

    sent = []

    def half(h):
        return pl.ds(0, CHUNK) if h is None else pl.ds(h * (CHUNK // 2), CHUNK // 2)

    def copy(q, dz, other, h, sem, dev):
        ref = spec.at[q, zat(dz) * 2 + (1 - core if other else core), half(h)]
        return pltpu.make_async_remote_copy(
            src_ref=ref, dst_ref=ref, send_sem=ag_s.at[q, sem], recv_sem=ag_r.at[q, sem],
            device_id=dev, device_id_type=MESH)

    def go(c):
        c.start()
        sent.append(c)

    def own(q):
        for h in range(2):
            go(copy(q, 0, False, h, h, right))
            go(copy(q, 0, False, h, 7 + h, left))
        go(copy(q, 0, False, None, 14, sib))

    def step(q, d, h):
        if d < 4 or h == 0:
            copy(q, -d, False, h, 2 * (d - 1) + h, right).wait_recv()
            if d < 3 or (d == 3 and h == 0):
                go(copy(q, -d, False, h, 2 * d + h, right))
        if d < 4 or h == 1:
            copy(q, d, False, h, 7 + (2 * (d - 1) + h if d < 4 else 6), left).wait_recv()
            if d < 3 or (d == 3 and h == 1):
                go(copy(q, d, False, h, 7 + (2 * d + h if d < 3 else 6), left))
        if d == 4:
            go(copy(q, 4, False, h, 21 + h, sib))
        elif h == 1:
            go(copy(q, -d, False, None, 14 + d, sib))
            go(copy(q, d, False, None, 17 + d, sib))

    def from_sib(q, d):
        if d == 0:
            copy(q, 0, True, None, 14, sib).wait_recv()
        elif d == 4:
            copy(q, 4, True, 0, 21, sib).wait_recv()
            copy(q, 4, True, 1, 22, sib).wait_recv()
        elif d < 0:
            copy(q, d, True, None, 14 - d, sib).wait_recv()
        else:
            copy(q, d, True, None, 17 + d, sib).wait_recv()

    def weights(d):
        zz = zat(d)

        @pl.loop(0, ROWS)
        def _(p):
            g = (gt[...] * li_ref[pl.ds(ROWS * t + p, 1), :]).astype(BF)
            w = dot(g, lf_ref[zz]).astype(BF)
            wmat[zz, pl.ds(pl.multiple_of(p * EMB, EMB), EMB), :] = w * lx[...]

    def apply(i, d, e, first=False):
        za, zb = zat(d), zat(e)
        g = jnp.concatenate([spec[i, pl.ds(zz * 2, 2)].reshape(2 * CHUNK, 256) for zz in (za, zb)], axis=0)

        @pl.loop(0, 3)
        def _(b):
            rows = pl.ds(pl.multiple_of(b * 512, 512), 512)
            v = dot(jnp.concatenate([wmat[za, rows, :], wmat[zb, rows, :]], axis=1), g)
            acc[i, rows, :] = v if first else acc[i, rows, :] + v

    c0 = math.sqrt(2.0 / math.pi)

    def member(e):
        @pl.loop(0, ROWS)
        def _(p):
            rows = pl.ds(pl.multiple_of(p * EMB, EMB), EMB)
            if e == 0:
                a = acc[0, rows, :]
            elif e == 2:
                a = jnp.concatenate([acc[1, rows, 128:], acc[2, rows, :128]], axis=1)
            else:
                head = half_turn(acc[0, rows, 128:] if e == 1 else acc[2, rows, :128])
                rest = half_turn(acc[1, rows, :128] if e == 1 else acc[2, rows, 128:])
                a = jnp.concatenate([jnp.where(low64e, head, rest), rest], axis=1)
            bk[p] = a.astype(BF)

        @pl.loop(0, 3)
        def _(it):
            lanes = pl.ds(pl.multiple_of(it * 768, 768), 768)
            x = x_ref[e, :, lanes]
            parts = []
            for k in range(3):
                n = 3 * it + k
                low = jnp.minimum(256 * n // 360, 4)
                parts.append(dot(jnp.concatenate([bk[low], bk[low + 1]], axis=1), iv_ref[n]))
            mixed = (jnp.concatenate(parts, axis=1) + dot(lt[...], x)).astype(BF)
            u = dot(w1t[...], mixed)
            h = 0.5 * u
            u = h * jnp.tanh(u * (c0 + (c0 * 0.044715) * (u * u))) + h
            outer = (mixed.astype(F32) + dot(w2t[...], u.astype(BF))).astype(BF)
            fs[e, :, lanes] = (x.astype(F32) + dot(rot[...], outer)).astype(BF)

        for i in range(1, nm):
            go(out_copy(e, i))
        field_ref[4 * m + e] = fs[e, :, pl.ds(pl.multiple_of(128 * m, 128), 256)]

    def out_copy(e, i):
        to = lax.rem(m + i, nm)
        return pltpu.make_async_remote_copy(
            src_ref=fs.at[e, :, pl.ds(pl.multiple_of(128 * to, 128), 256)], dst_ref=field_ref.at[4 * m + e],
            send_sem=ax_s.at[e, i], recv_sem=ax_r.at[e, i], device_id=(to, t), device_id_type=MESH)

    spectra((0,))
    pl.semaphore_wait(bar, nt + nm - 2)
    own(0)
    spectra((1, 2))
    lv = jnp.concatenate([lift_ref[...].astype(F32), jnp.zeros((CPAD - VARS, EMB), F32)], axis=0).T.astype(BF)
    lt[...] = lv
    lx[...] = dot(lv[:, :VARS], sp_ref[...]).astype(BF)
    gt[...] = gain_ref[...].T
    weights(1)
    weights(-1)
    step(0, 1, 0)
    weights(2)
    step(0, 1, 1)
    own(1)
    weights(-2)
    step(0, 2, 0)
    weights(3)
    step(0, 2, 1)
    weights(-3)
    from_sib(0, 1)
    from_sib(0, -1)
    apply(0, 1, -1, True)
    step(0, 3, 0)
    weights(0)
    step(0, 3, 1)
    from_sib(0, 2)
    from_sib(0, -2)
    apply(0, 2, -2)
    step(0, 4, 0)
    step(0, 4, 1)
    weights(4)
    step(1, 1, 0)
    step(1, 1, 1)
    own(2)
    from_sib(0, 3)
    from_sib(0, -3)
    apply(0, 3, -3)
    step(1, 2, 0)
    from_sib(0, 0)
    from_sib(0, 4)
    apply(0, 0, 4)
    step(1, 2, 1)
    w1t[...] = w1_ref[...].astype(F32).T.astype(BF)
    w2t[...] = w2_ref[...].astype(F32).T.astype(BF)
    rot[...] = jnp.concatenate([ro_ref[...].astype(F32), jnp.zeros((CPAD - VARS, EMB), F32)], axis=0).astype(BF)
    from_sib(1, 1)
    from_sib(1, -1)
    apply(1, 1, -1, True)
    step(1, 3, 0)
    from_sib(1, 2)
    from_sib(1, -2)
    apply(1, 2, -2)
    step(1, 3, 1)
    step(1, 4, 0)
    step(1, 4, 1)
    step(2, 1, 0)
    member(0)
    step(2, 1, 1)
    from_sib(1, 3)
    from_sib(1, -3)
    apply(1, 3, -3)
    step(2, 2, 0)
    from_sib(1, 0)
    from_sib(1, 4)
    apply(1, 0, 4)
    step(2, 2, 1)
    from_sib(2, 1)
    from_sib(2, -1)
    apply(2, 1, -1, True)
    step(2, 3, 0)
    step(2, 3, 1)
    member(1)
    step(2, 4, 0)
    step(2, 4, 1)
    from_sib(2, 2)
    from_sib(2, -2)
    apply(2, 2, -2)
    from_sib(2, 3)
    from_sib(2, -3)
    apply(2, 3, -3)
    from_sib(2, 0)
    from_sib(2, 4)
    apply(2, 0, 4)
    member(2)
    member(3)

    cells = cell_ref[...] + 7 * m
    pick = (lax.broadcasted_iota(jnp.int32, (256, 128), 0) == cells).astype(BF)
    nt_dims = (((1,), (1,)), ((), ()))
    op = jnp.concatenate([op_ref[...].reshape(VARS, 128), jnp.zeros((CPAD - VARS, 128), F32)], axis=0)

    def counterparts(e, src):
        f = 4 * src + e
        v = dot(field_ref[f], pick) * op
        cp[pl.ds(f, 1), :] = jnp.sum(v, axis=0, keepdims=True)

    for e in range(4):
        for i in range(nm):
            if i:
                out_copy(e, i).wait_recv()
            counterparts(e, lax.rem(m - i + nm, nm))
    c = cp[...]
    n = c.shape[0]
    ybar = jnp.mean(c, axis=0, keepdims=True)
    spread = c - ybar
    live = lax.broadcasted_iota(jnp.int32, (1, 128), 1) < count_ref[...]
    weight = jnp.where(live, 1.0 / err_ref[...], 0.0)
    both = jnp.concatenate([spread, val_ref[...] - ybar, jnp.zeros((127 - n, 128), F32)], axis=0)
    gram = lax.dot_general(spread * weight, both, nt_dims, precision=HI, preferred_element_type=F32)
    per = n // nt
    for b in range(nt):
        part[b, :per] = gram[per * b:per * b + per]
        part[b, per:] = jnp.zeros((8 - per, 128), F32)

    def send(src, dst, phase, i, dev):
        cc = pltpu.make_async_remote_copy(
            src_ref=src, dst_ref=dst, send_sem=rs_s.at[phase, i], recv_sem=rs_r.at[phase, i],
            device_id=dev, device_id_type=MESH)
        go(cc)
        return cc

    def turned(g):
        @pl.loop(0, 16)
        def _(k):
            turn[k, :, :CPAD] = field_ref[16 * g + k].astype(F32).T

        for hf in range(2):
            v = turn[8 * hf:8 * hf + 8, pl.ds(7 * m, NCELL), :]
            stage[:, 8 * hf:8 * hf + 8, :] = jnp.transpose(v, (1, 0, 2))
        ft_ref[:, 16 * g:16 * g + 16, :] = stage[...].astype(BF)

    one = [send(part.at[lax.rem(t + i, nt)], got.at[i], 0, i, tile_peer(i)) for i in range(1, nt)]
    turned(0)
    tot = part[t]
    for cc in one:
        cc.wait_recv()
    for i in range(1, nt):
        tot = tot + got[i]
    mid[...] = tot
    two = [send(mid, midg.at[m], 1, i, member_peer(i)) for i in range(1, nm)]
    midg[m] = tot
    turned(1)
    for cc in two:
        cc.wait_recv()
    tot = midg[0]
    for i in range(1, nm):
        tot = tot + midg[i]
    stats_ref[t] = tot
    fin[...] = tot
    three = [send(fin, stats_ref.at[t], 2, i, tile_peer(i)) for i in range(1, nt)]
    turned(2)
    turned(3)
    for cc in three:
        cc.wait_recv()
    for cc in sent:
        cc.wait_send()


def forecast_call(args, nm, nt, n):
    vm = pl.BlockSpec(memory_space=pltpu.VMEM)
    dma = pltpu.SemaphoreType.DMA
    return pl.pallas_call(
        functools.partial(forecast_kernel, nm),
        out_shape=[jax.ShapeDtypeStruct((NCELL, n, 128), BF), jax.ShapeDtypeStruct((nt, 8, 128), F32)],
        in_specs=[vm] * len(args),
        out_specs=[vm, vm],
        scratch_shapes=[
            pltpu.VMEM((3, nt, CHUNK, 256), BF),
            pltpu.VMEM((NZ, ROWS * EMB, 2 * CHUNK), BF),
            pltpu.VMEM((3, ROWS * EMB, 256), F32),
            pltpu.VMEM((ROWS, EMB, 256), BF),
            pltpu.VMEM((4, CPAD, CELLS), BF),
            pltpu.VMEM((n, CPAD, 256), BF),
            pltpu.VMEM((n, 128), F32),
            pltpu.VMEM((EMB, 2 * CHUNK), BF),
            pltpu.VMEM((EMB, CPAD), BF),
            pltpu.VMEM((HID, EMB), BF),
            pltpu.VMEM((EMB, HID), BF),
            pltpu.VMEM((CPAD, EMB), BF),
            pltpu.VMEM((EMB, NLAT), F32),
            pltpu.VMEM((16, 256, 128), F32),
            pltpu.VMEM((NCELL, 16, 128), F32),
            pltpu.VMEM((nt, 8, 128), F32),
            pltpu.VMEM((nt, 8, 128), F32),
            pltpu.VMEM((8, 128), F32),
            pltpu.VMEM((nm, 8, 128), F32),
            pltpu.VMEM((8, 128), F32),
            dma((3, 23)), dma((3, 23)), dma((4, 16)), dma((4, 16)), dma((3, 16)), dma((3, 16)),
        ],
        compiler_params=pltpu.CompilerParams(
            collective_id=0, has_side_effects=True, vmem_limit_bytes=62 * 2**20),
        name="forecast",
    )(*args)


def mix_of(stats, n):
    rows = lax.broadcasted_iota(jnp.int32, (n, n), 0)
    cols = lax.broadcasted_iota(jnp.int32, (n, n), 1)
    eye = (rows == cols).astype(F32)
    rw = lax.broadcasted_iota(jnp.int32, (n, 128), 0)
    cw = lax.broadcasted_iota(jnp.int32, (n, 128), 1)
    wide = jnp.where(cw < n, stats / (n - 1.0) + (rw == cw).astype(F32), stats)
    system = wide[:, :n]
    scale = jnp.sqrt(jnp.sum(system * system))
    up, root = system / scale, eye
    done = 0
    for it in range(NS_ITERS):
        shift = 1.5 * eye - 0.5 * jnp.dot(root, up, precision=HI, preferred_element_type=F32)
        up = jnp.dot(up, shift, precision=HI, preferred_element_type=F32)
        root = jnp.dot(shift, root, precision=HI, preferred_element_type=F32)
        upto = min(n, -(-n * (it + 1) // NS_ITERS))
        for j in range(done, upto):
            r = wide[j:j + 1, :]
            r = r / wide[j:j + 1, j:j + 1]
            col = wide[:, j:j + 1] - (rw[:, :1] == j).astype(F32)
            wide = wide - col * r
        done = upto
    weight = wide[:, n:n + 1] / (n - 1.0)
    return root / jnp.sqrt(scale) + weight


def analysis_kernel(stats_ref, ft_ref, out_ref, dev, mean):
    n = ft_ref.shape[1]
    nt = stats_ref.shape[0]
    step = 9

    @pl.loop(0, NCELL // step)
    def _(i):
        for k in range(step):
            v = ft_ref[i * step + k].astype(F32)
            bar = jnp.mean(v, axis=0, keepdims=True)
            mean[i * step + k] = bar
            dev[i * step + k] = (v - bar).astype(BF)

    stats = jnp.concatenate([stats_ref[b, :n // nt] for b in range(nt)], axis=0)
    mix = mix_of(stats, n).T
    hi = mix.astype(BF)
    lo = (mix - hi.astype(F32)).astype(BF)
    both = jnp.concatenate([hi, lo], axis=1)

    @pl.loop(0, NCELL // step)
    def _(i):
        d = jnp.concatenate([dev[i * step + k] for k in range(step)], axis=1)
        v = dot(both, jnp.concatenate([d, d], axis=0))
        for k in range(step):
            out_ref[i * step + k] = (v[:, 128 * k:128 * k + VARS] + mean[i * step + k][:, :VARS]).astype(BF)


def analysis_call(stats, ft):
    vm = pl.BlockSpec(memory_space=pltpu.VMEM)
    n = ft.shape[1]
    return pl.pallas_call(
        analysis_kernel,
        out_shape=jax.ShapeDtypeStruct((NCELL, n, VARS), BF),
        in_specs=[vm, vm],
        out_specs=vm,
        scratch_shapes=[pltpu.VMEM((NCELL, n, 128), BF), pltpu.VMEM((NCELL, 1, 128), F32)],
        compiler_params=pltpu.CompilerParams(vmem_limit_bytes=40 * 2**20),
        name="analysis",
    )(stats, ft)


def shards(x, lift, gain, w1, w2, readout, obs_count, obs_cell, obs_op, obs_value, obs_error):
    mem, nvar, rows, nlon = x.shape
    nt, nm = lax.axis_size("tile"), lax.axis_size("member")
    tables = (jnp.asarray(a) for a in kernel_tables())
    xk = jnp.pad(x.reshape(mem, nvar, rows * nlon), ((0, 0), (0, CPAD - nvar), (0, CELLS - rows * nlon)))
    args = (xk, *tables, gain.T, lift, w1, w2, readout.T,
            obs_count.reshape(1, 1), obs_cell, obs_op.transpose(2, 0, 1), obs_value, obs_error)
    ft, stats = forecast_call(args, nm, nt, mem * nm)
    return jnp.transpose(analysis_call(stats, ft), (2, 0, 1))


def solution(mesh):
    placed = (
        P("member", None, "tile", None),
        P(), P(), P(), P(), P(),
        P(("tile", "member")),
        P(("tile", "member"), None),
        P(("tile", "member"), None, None),
        P(("tile", "member"), None),
        P(("tile", "member"), None),
    )
    return jax.shard_map(
        shards, mesh=mesh, in_specs=placed, out_specs=P(None, ("tile", "member"), None), check_vma=False)
```

```python
import functools
import math

import jax
import jax.numpy as jnp
import numpy as np
from jax import lax
from jax.experimental import pallas as pl
from jax.experimental.pallas import tpu as pltpu
from jax.sharding import PartitionSpec as P

MMAX = 96
NS_ITERS = 24
BF = jnp.bfloat16
F32 = jnp.float32
HI = lax.Precision.HIGHEST
MESH = pl.DeviceIdType.MESH


def lon_tables(nlon, mmax):
    lon = np.arange(nlon, dtype=np.float64)
    wave = np.arange(mmax, dtype=np.float64)
    phase = np.mod(lon[:, None] * wave[None, :], float(nlon))
    angle = 2.0 * math.pi * phase / nlon
    forward = np.concatenate([np.cos(angle), -np.sin(angle)], axis=1)
    factor = np.where(wave == 0.0, 1.0, 2.0) / nlon
    inverse = np.concatenate([np.cos(angle) * factor, -np.sin(angle) * factor], axis=1).T
    return (forward.astype(np.float32).astype(BF), inverse.astype(np.float32).astype(BF))


def lat_tables(nlat):
    row = np.arange(nlat, dtype=np.float64)
    phase = np.mod((2.0 * row[:, None] + 1.0) * row[None, :], float(4 * nlat))
    basis = np.cos(math.pi * phase / (2.0 * nlat))
    factor = np.where(row == 0.0, 1.0, 2.0) / nlat
    forward = (basis * factor[None, :]).T
    return (forward.astype(np.float32).astype(BF), basis.astype(np.float32).astype(BF))


VARS, CPAD = 73, 80
ROWS, NLON, NLAT = 6, 360, 96
KCOL = 2 * MMAX
CHUNK = 448
CELLS = 2304
EMB, HID = 256, 512
NZ = 8
NCELL = 135


def chunk_index():
    lat = np.full(CHUNK, -1)
    chan = np.full(CHUNK, -1)
    for p in range(ROWS):
        lat[64 * p:64 * p + 64], chan[64 * p:64 * p + 64] = p, np.arange(64)
        at = 384 + 9 * p
        lat[at:at + 9], chan[at:at + 9] = p, np.arange(64, 73)
    return lat, chan


def window(p):
    start = 128 * (360 * p // 128)
    return start, min(512, CELLS - start)


def kernel_tables():
    lon_f, lon_i = (np.asarray(a).astype(np.float32) for a in lon_tables(NLON, MMAX))
    lat_f, lat_i = (np.asarray(a).astype(np.float32) for a in lat_tables(NLAT))
    fw = np.zeros((ROWS, 512, 256), np.float32)
    for p in range(ROWS):
        at = 360 * p - window(p)[0]
        fw[p, at:at + 360, :KCOL] = lon_f
    iv = np.zeros((9, 2, 256, 256), np.float32)
    for n in range(9):
        low = min(256 * n // 360, 4)
        for s in range(2):
            for col in range(256):
                q = 256 * n + col - 360 * (low + s)
                if 0 <= q < 360:
                    iv[n, s, :KCOL, col] = lon_i[:, q]
    lat, chan = chunk_index()
    lf = np.zeros((16, NLAT, CHUNK), np.float32)
    for t in range(16):
        lf[t] = lat_f[:, 6 * t + np.maximum(lat, 0)] * (lat >= 0)
    lf = lf.reshape(NZ, 2, NLAT, CHUNK).transpose(0, 2, 1, 3).reshape(NZ, NLAT, 2 * CHUNK)
    spread = (chan[None, :] == np.arange(VARS)[:, None]).astype(np.float32)
    spread = np.concatenate([spread, spread], axis=1)
    return fw.astype(BF), iv.reshape(9, 512, 256).astype(BF), lf.astype(BF), lat_i, spread.astype(BF)


def dot(a, b):
    return jnp.dot(a, b, preferred_element_type=F32)


def forecast_kernel(nm, x_ref, fw_ref, iv_ref, lf_ref, li_ref, sp_ref, gain_ref, lift_ref, w1_ref, w2_ref, ro_ref,
                    count_ref, cell_ref, op_ref, val_ref, err_ref,
                    ft_ref, stats_ref,
                    spec, wmat, acc, bk, fs, field_ref, cp, lx, lt, w1t, w2t, rot, gt, turn, stage, part, got, mid, midg, fin,
                    ag_s, ag_r, ax_s, ax_r, rs_s, rs_r):
    m, t = lax.axis_index("member"), lax.axis_index("tile")
    nt = 2 * NZ
    z, core = t // 2, lax.rem(t, 2)

    def zat(d):
        return lax.rem(z + d + NZ, NZ)

    def member_peer(i):
        return (lax.rem(m + i, nm), t)

    def tile_peer(i):
        return (m, lax.rem(t + i, nt))

    right, left, sib = (m, zat(1) * 2 + core), (m, zat(-1) * 2 + core), (m, z * 2 + 1 - core)
    bar = pltpu.get_barrier_semaphore()
    for i in range(1, nt):
        pl.semaphore_signal(bar, inc=1, device_id=tile_peer(i), device_id_type=MESH)
    for i in range(1, nm):
        pl.semaphore_signal(bar, inc=1, device_id=member_peer(i), device_id_type=MESH)

    low64 = lax.broadcasted_iota(jnp.int32, (CPAD, 128), 1) < 64
    low64e = lax.broadcasted_iota(jnp.int32, (EMB, 128), 1) < 64

    def half_turn(v):
        return pltpu.roll(v, 64, 1)

    def spectra(pieces):
        tails = {i: [] for i in pieces}
        for p in range(ROWS):
            at, wide = window(p)

            def both(e):
                v = dot(x_ref[e, :, at:at + wide], fw_ref[p, :wide])
                return v[:, :128], v[:, 128:]

            for i in pieces:
                if i == 0:
                    (a0, b0), (a1, _) = both(0), both(1)
                    v = [a0, jnp.where(low64, b0, half_turn(a1))]
                elif i == 1:
                    (a1, b1), (a2, _) = both(1), both(2)
                    v = [jnp.where(low64, half_turn(a1), half_turn(b1)), a2]
                else:
                    (_, b2), (a3, b3) = both(2), both(3)
                    a3 = half_turn(a3)
                    v = [jnp.where(low64, b2, a3), jnp.where(low64, a3, half_turn(b3))]
                v = jnp.concatenate(v, axis=1)
                spec[i, t, 64 * p:64 * p + 64] = v[:64].astype(BF)
                tails[i].append(v[64:VARS])
        for i in pieces:
            tails[i].append(jnp.zeros((10, 256), F32))
            spec[i, t, 384:CHUNK] = jnp.concatenate(tails[i], axis=0).astype(BF)

    sent = []

    def copy(q, dz, other, h, sem, dev):
        rows = pl.ds(0, CHUNK) if h is None else pl.ds(h * (CHUNK // 2), CHUNK // 2)
        ref = spec.at[q, zat(dz) * 2 + (1 - core if other else core), rows]
        return pltpu.make_async_remote_copy(
            src_ref=ref, dst_ref=ref, send_sem=ag_s.at[q, sem], recv_sem=ag_r.at[q, sem],
            device_id=dev, device_id_type=MESH)

    def go(c):
        c.start()
        sent.append(c)

    def own(q):
        go(copy(q, 0, False, None, 0, right))
        go(copy(q, 0, False, None, 4, left))
        go(copy(q, 0, False, None, 8, sib))

    def step(q, d):
        for sign, base, h, dev in ((-1, 0, 0, right), (1, 4, 1, left)):
            copy(q, sign * d, False, h if d == 4 else None, base + d - 1, dev).wait_recv()
            if d < 4:
                go(copy(q, sign * d, False, h if d == 3 else None, base + d, dev))
        for sign, base, h in ((-1, 8, 0), (1, 12, 1)):
            go(copy(q, sign * d, False, h if d == 4 else None, base + d, sib))

    def from_sib(q, d):
        if d == 0:
            copy(q, 0, True, None, 8, sib).wait_recv()
        elif d == 4:
            copy(q, 4, True, 0, 12, sib).wait_recv()
            copy(q, 4, True, 1, 16, sib).wait_recv()
        else:
            copy(q, d, True, None, 8 - d if d < 0 else 12 + d, sib).wait_recv()

    def weights(d):
        zz = zat(d)

        @pl.loop(0, ROWS)
        def _(p):
            g = (gt[...] * li_ref[pl.ds(ROWS * t + p, 1), :]).astype(BF)
            w = dot(g, lf_ref[zz]).astype(BF)
            wmat[zz, pl.ds(pl.multiple_of(p * EMB, EMB), EMB), :] = w * lx[...]

    def apply(i, d, e, first=False):
        za, zb = zat(d), zat(e)
        g = jnp.concatenate([spec[i, pl.ds(zz * 2, 2)].reshape(2 * CHUNK, 256) for zz in (za, zb)], axis=0)

        @pl.loop(0, 3)
        def _(b):
            rows = pl.ds(pl.multiple_of(b * 512, 512), 512)
            v = dot(jnp.concatenate([wmat[za, rows, :], wmat[zb, rows, :]], axis=1), g)
            acc[i, rows, :] = v if first else acc[i, rows, :] + v

    c0 = math.sqrt(2.0 / math.pi)

    def member(e):
        @pl.loop(0, ROWS)
        def _(p):
            rows = pl.ds(pl.multiple_of(p * EMB, EMB), EMB)
            if e == 0:
                a = acc[0, rows, :]
            elif e == 2:
                a = jnp.concatenate([acc[1, rows, 128:], acc[2, rows, :128]], axis=1)
            else:
                head = half_turn(acc[0, rows, 128:] if e == 1 else acc[2, rows, :128])
                rest = half_turn(acc[1, rows, :128] if e == 1 else acc[2, rows, 128:])
                a = jnp.concatenate([jnp.where(low64e, head, rest), rest], axis=1)
            bk[p] = a.astype(BF)

        @pl.loop(0, 3)
        def _(it):
            lanes = pl.ds(pl.multiple_of(it * 768, 768), 768)
            x = x_ref[e, :, lanes]
            parts = []
            for k in range(3):
                n = 3 * it + k
                low = jnp.minimum(256 * n // 360, 4)
                parts.append(dot(jnp.concatenate([bk[low], bk[low + 1]], axis=1), iv_ref[n]))
            mixed = (jnp.concatenate(parts, axis=1) + dot(lt[...], x)).astype(BF)
            u = dot(w1t[...], mixed)
            h = 0.5 * u
            u = h * jnp.tanh(u * (c0 + (c0 * 0.044715) * (u * u))) + h
            outer = (mixed.astype(F32) + dot(w2t[...], u.astype(BF))).astype(BF)
            fs[e, :, lanes] = (x.astype(F32) + dot(rot[...], outer)).astype(BF)

        for i in range(1, nm):
            go(out_copy(e, i))
        field_ref[nm * e + m] = fs[e, :, pl.ds(pl.multiple_of(128 * m, 128), 256)]

    def out_copy(e, i):
        to = lax.rem(m + i, nm)
        return pltpu.make_async_remote_copy(
            src_ref=fs.at[e, :, pl.ds(pl.multiple_of(128 * to, 128), 256)], dst_ref=field_ref.at[nm * e + m],
            send_sem=ax_s.at[e, i], recv_sem=ax_r.at[e, i], device_id=(to, t), device_id_type=MESH)

    spectra((0,))
    pl.semaphore_wait(bar, nt + nm - 2)
    own(0)
    spectra((1,))
    own(1)
    spectra((2,))
    lv = jnp.concatenate([lift_ref[...].astype(F32), jnp.zeros((CPAD - VARS, EMB), F32)], axis=0).T.astype(BF)
    lt[...] = lv
    lx[...] = dot(lv[:, :VARS], sp_ref[...]).astype(BF)
    gt[...] = gain_ref[...].T
    weights(1)
    weights(-1)
    weights(2)
    weights(-2)
    step(0, 1)
    weights(3)
    step(1, 1)
    weights(-3)
    weights(0)
    from_sib(0, 1)
    from_sib(0, -1)
    apply(0, 1, -1, True)
    step(0, 2)
    own(2)
    weights(4)
    from_sib(1, 1)
    from_sib(1, -1)
    apply(1, 1, -1, True)
    step(1, 2)
    from_sib(0, 2)
    from_sib(0, -2)
    apply(0, 2, -2)
    step(0, 3)
    from_sib(1, 2)
    from_sib(1, -2)
    apply(1, 2, -2)
    step(2, 1)
    w1t[...] = w1_ref[...].astype(F32).T.astype(BF)
    w2t[...] = w2_ref[...].astype(F32).T.astype(BF)
    rot[...] = jnp.concatenate([ro_ref[...].astype(F32), jnp.zeros((CPAD - VARS, EMB), F32)], axis=0).astype(BF)
    step(1, 3)
    from_sib(0, 3)
    from_sib(0, -3)
    apply(0, 3, -3)
    step(0, 4)
    from_sib(1, 3)
    from_sib(1, -3)
    apply(1, 3, -3)
    step(1, 4)
    from_sib(0, 0)
    from_sib(0, 4)
    apply(0, 0, 4)
    step(2, 2)
    member(0)
    from_sib(2, 1)
    from_sib(2, -1)
    apply(2, 1, -1, True)
    step(2, 3)
    from_sib(1, 0)
    from_sib(1, 4)
    apply(1, 0, 4)
    from_sib(2, 2)
    from_sib(2, -2)
    apply(2, 2, -2)
    step(2, 4)
    member(1)
    from_sib(2, 3)
    from_sib(2, -3)
    apply(2, 3, -3)
    from_sib(2, 0)
    from_sib(2, 4)
    apply(2, 0, 4)
    member(2)
    member(3)

    cells = cell_ref[...] + 7 * m
    pick = (lax.broadcasted_iota(jnp.int32, (256, 128), 0) == cells).astype(BF)
    nt_dims = (((1,), (1,)), ((), ()))
    op = jnp.concatenate([op_ref[...].reshape(VARS, 128), jnp.zeros((CPAD - VARS, 128), F32)], axis=0)

    def counterparts(e, src):
        f = nm * e + src
        v = dot(field_ref[f], pick) * op
        cp[pl.ds(f, 1), :] = jnp.sum(v, axis=0, keepdims=True)

    def turned(g):
        @pl.loop(0, 16)
        def _(k):
            turn[k, :, :CPAD] = field_ref[16 * g + k].astype(F32).T

        for hf in range(2):
            v = turn[8 * hf:8 * hf + 8, pl.ds(7 * m, NCELL), :]
            stage[:, 8 * hf:8 * hf + 8, :] = jnp.transpose(v, (1, 0, 2))
        ft_ref[:, 16 * g:16 * g + 16, :] = stage[...].astype(BF)

    def collect(e):
        for i in range(nm):
            if i:
                out_copy(e, i).wait_recv()
            counterparts(e, lax.rem(m - i + nm, nm))

    for e in range(3):
        collect(e)
        turned(e)
    for cc in sent:
        cc.wait_send()
    sent.clear()
    collect(3)
    c = cp[...]
    n = c.shape[0]
    ybar = jnp.mean(c, axis=0, keepdims=True)
    spread = c - ybar
    live = lax.broadcasted_iota(jnp.int32, (1, 128), 1) < count_ref[...]
    weight = jnp.where(live, 1.0 / err_ref[...], 0.0)
    both = jnp.concatenate([spread, val_ref[...] - ybar, jnp.zeros((127 - n, 128), F32)], axis=0)
    gram = lax.dot_general(spread * weight, both, nt_dims, precision=HI, preferred_element_type=F32)
    per = n // nt
    for b in range(nt):
        part[b, :per] = gram[per * b:per * b + per]
        part[b, per:] = jnp.zeros((8 - per, 128), F32)

    def send(src, dst, phase, i, dev):
        cc = pltpu.make_async_remote_copy(
            src_ref=src, dst_ref=dst, send_sem=rs_s.at[phase, i], recv_sem=rs_r.at[phase, i],
            device_id=dev, device_id_type=MESH)
        go(cc)
        return cc

    one = [send(part.at[lax.rem(t + i, nt)], got.at[i], 0, i, tile_peer(i)) for i in range(1, nt)]
    turned(3)
    tot = part[t]
    for cc in one:
        cc.wait_recv()
    for i in range(1, nt):
        tot = tot + got[i]
    mid[...] = tot
    two = [send(mid, midg.at[m], 1, i, member_peer(i)) for i in range(1, nm)]
    midg[m] = tot
    for cc in two:
        cc.wait_recv()
    tot = midg[0]
    for i in range(1, nm):
        tot = tot + midg[i]
    stats_ref[t] = tot
    fin[...] = tot
    three = [send(fin, stats_ref.at[t], 2, i, tile_peer(i)) for i in range(1, nt)]
    for cc in three:
        cc.wait_recv()
    for cc in sent:
        cc.wait_send()


def forecast_call(args, nm, nt, n):
    vm = pl.BlockSpec(memory_space=pltpu.VMEM)
    dma = pltpu.SemaphoreType.DMA
    return pl.pallas_call(
        functools.partial(forecast_kernel, nm),
        out_shape=[jax.ShapeDtypeStruct((NCELL, n, 128), BF), jax.ShapeDtypeStruct((nt, 8, 128), F32)],
        in_specs=[vm] * len(args),
        out_specs=[vm, vm],
        scratch_shapes=[
            pltpu.VMEM((3, nt, CHUNK, 256), BF),
            pltpu.VMEM((NZ, ROWS * EMB, 2 * CHUNK), BF),
            pltpu.VMEM((3, ROWS * EMB, 256), F32),
            pltpu.VMEM((ROWS, EMB, 256), BF),
            pltpu.VMEM((4, CPAD, CELLS), BF),
            pltpu.VMEM((n, CPAD, 256), BF),
            pltpu.VMEM((n, 128), F32),
            pltpu.VMEM((EMB, 2 * CHUNK), BF),
            pltpu.VMEM((EMB, CPAD), BF),
            pltpu.VMEM((HID, EMB), BF),
            pltpu.VMEM((EMB, HID), BF),
            pltpu.VMEM((CPAD, EMB), BF),
            pltpu.VMEM((EMB, NLAT), F32),
            pltpu.VMEM((16, 256, 128), F32),
            pltpu.VMEM((NCELL, 16, 128), F32),
            pltpu.VMEM((nt, 8, 128), F32),
            pltpu.VMEM((nt, 8, 128), F32),
            pltpu.VMEM((8, 128), F32),
            pltpu.VMEM((nm, 8, 128), F32),
            pltpu.VMEM((8, 128), F32),
            dma((3, 17)), dma((3, 17)), dma((4, 16)), dma((4, 16)), dma((3, 16)), dma((3, 16)),
        ],
        compiler_params=pltpu.CompilerParams(
            collective_id=0, has_side_effects=True, vmem_limit_bytes=62 * 2**20),
        name="forecast",
    )(*args)


def split(a):
    hi = a.astype(BF)
    rest = a - hi.astype(F32)
    mid = rest.astype(BF)
    return hi, mid, (rest - mid.astype(F32)).astype(BF)


def mix_of(stats, n):
    rw = lax.broadcasted_iota(jnp.int32, (n, 128), 0)
    cw = lax.broadcasted_iota(jnp.int32, (n, 128), 1)
    low = cw < n
    wide = jnp.where(low, stats / (n - 1.0) + (rw == cw).astype(F32), stats)
    eye = ((rw == cw) | (rw + n == cw)).astype(F32)
    system = jnp.where(low, wide, pltpu.roll(wide, n, 1))
    scale = jnp.sqrt(0.5 * jnp.sum(system * system))

    def left(parts):
        hi, mid, lo = (v.astype(F32) for v in parts)
        return jnp.concatenate(
            [parts[0], jnp.where(low, mid, hi).astype(BF), jnp.where(low, lo, mid).astype(BF)], axis=1)

    def right(parts):
        hi, mid, lo = parts
        return jnp.concatenate([hi, mid, hi, lo, hi, mid], axis=0)

    up, root = system / scale, eye
    done = 0
    for it in range(NS_ITERS):
        su, sr = split(up), split(root)
        shift = 1.5 * eye - 0.5 * dot(left(sr), right(su))
        ss = split(shift)
        up = dot(left(su), right(ss))
        root = dot(left(ss), right(sr))
        upto = min(n, -(-n * (it + 1) // NS_ITERS))
        for j in range(done, upto):
            r = wide[j:j + 1, :]
            r = r / wide[j:j + 1, j:j + 1]
            col = wide[:, j:j + 1] - (rw[:, :1] == j).astype(F32)
            wide = wide - col * r
        done = upto
    weight = wide[:, n:n + 1] / (n - 1.0)
    return root[:, :n] / jnp.sqrt(scale) + weight


def analysis_kernel(stats_ref, field_ref, out_ref, ft, sem):
    n = ft.shape[1]
    nt = stats_ref.shape[0]
    load = pltpu.make_async_copy(field_ref, ft, sem)
    load.start()
    stats = jnp.concatenate([stats_ref[b, :n // nt] for b in range(nt)], axis=0)
    mix = mix_of(stats, n)
    mix = (mix + (1.0 - jnp.sum(mix, axis=0, keepdims=True)) / n).T
    hi = mix.astype(BF)
    lo = (mix - hi.astype(F32)).astype(BF)
    rows = lax.broadcasted_iota(jnp.int32, (n, n), 0)
    cols = lax.broadcasted_iota(jnp.int32, (n, n), 1)
    order = (cols == (n // 4) * (rows & 3) + (rows >> 2)).astype(BF)
    both = dot(order, jnp.concatenate([hi, lo], axis=1)).astype(BF)
    load.wait()
    step = 9

    @pl.loop(0, NCELL // step)
    def _(i):
        f = jnp.concatenate([ft[i * step + k] for k in range(step)], axis=1)
        v = dot(both, jnp.concatenate([f, f], axis=0))
        for k in range(step):
            out_ref[i * step + k] = v[:, 128 * k:128 * k + VARS].astype(BF)


def analysis_call(stats, ft):
    vm = pl.BlockSpec(memory_space=pltpu.VMEM)
    n = ft.shape[1]
    return pl.pallas_call(
        analysis_kernel,
        out_shape=jax.ShapeDtypeStruct((NCELL, n, VARS), BF),
        in_specs=[vm, pl.BlockSpec(memory_space=pl.ANY)],
        out_specs=vm,
        scratch_shapes=[pltpu.VMEM((NCELL, n, 128), BF), pltpu.SemaphoreType.DMA],
        compiler_params=pltpu.CompilerParams(vmem_limit_bytes=40 * 2**20),
        name="analysis",
    )(stats, ft)


def shards(x, lift, gain, w1, w2, readout, obs_count, obs_cell, obs_op, obs_value, obs_error):
    mem, nvar, rows, nlon = x.shape
    nt, nm = lax.axis_size("tile"), lax.axis_size("member")
    tables = (jnp.asarray(a) for a in kernel_tables())
    xk = jnp.pad(x.reshape(mem, nvar, rows * nlon), ((0, 0), (0, CPAD - nvar), (0, CELLS - rows * nlon)))
    args = (xk, *tables, gain.T, lift, w1, w2, readout.T,
            obs_count.reshape(1, 1), obs_cell, obs_op.transpose(2, 0, 1), obs_value, obs_error)
    ft, stats = forecast_call(args, nm, nt, mem * nm)
    return jnp.transpose(analysis_call(stats, ft), (2, 0, 1))


def solution(mesh):
    placed = (
        P("member", None, "tile", None),
        P(), P(), P(), P(), P(),
        P(("tile", "member")),
        P(("tile", "member"), None),
        P(("tile", "member"), None, None),
        P(("tile", "member"), None),
        P(("tile", "member"), None),
    )
    return jax.shard_map(
        shards, mesh=mesh, in_specs=placed, out_specs=P(None, ("tile", "member"), None), check_vma=False)
```

```python
import functools
import math

import jax
import jax.numpy as jnp
import numpy as np
from jax import lax
from jax.experimental import pallas as pl
from jax.experimental.pallas import tpu as pltpu
from jax.sharding import PartitionSpec as P

MMAX = 96
NS_ITERS = 24
BF = jnp.bfloat16
F32 = jnp.float32
HI = lax.Precision.HIGHEST
MESH = pl.DeviceIdType.MESH


def lon_tables(nlon, mmax):
    lon = np.arange(nlon, dtype=np.float64)
    wave = np.arange(mmax, dtype=np.float64)
    phase = np.mod(lon[:, None] * wave[None, :], float(nlon))
    angle = 2.0 * math.pi * phase / nlon
    forward = np.concatenate([np.cos(angle), -np.sin(angle)], axis=1)
    factor = np.where(wave == 0.0, 1.0, 2.0) / nlon
    inverse = np.concatenate([np.cos(angle) * factor, -np.sin(angle) * factor], axis=1).T
    return (forward.astype(np.float32).astype(BF), inverse.astype(np.float32).astype(BF))


def lat_tables(nlat):
    row = np.arange(nlat, dtype=np.float64)
    phase = np.mod((2.0 * row[:, None] + 1.0) * row[None, :], float(4 * nlat))
    basis = np.cos(math.pi * phase / (2.0 * nlat))
    factor = np.where(row == 0.0, 1.0, 2.0) / nlat
    forward = (basis * factor[None, :]).T
    return (forward.astype(np.float32).astype(BF), basis.astype(np.float32).astype(BF))


VARS, CPAD = 73, 80
ROWS, NLON, NLAT = 6, 360, 96
KCOL = 2 * MMAX
CHUNK = 448
CELLS = 2304
EMB, HID = 256, 512
NZ = 8
NCELL = 135


def chunk_index():
    lat = np.full(CHUNK, -1)
    chan = np.full(CHUNK, -1)
    for p in range(ROWS):
        lat[64 * p:64 * p + 64], chan[64 * p:64 * p + 64] = p, np.arange(64)
        at = 384 + 9 * p
        lat[at:at + 9], chan[at:at + 9] = p, np.arange(64, 73)
    return lat, chan


def kernel_tables():
    lon_f, lon_i = (np.asarray(a).astype(np.float32) for a in lon_tables(NLON, MMAX))
    lat_f, lat_i = (np.asarray(a).astype(np.float32) for a in lat_tables(NLAT))
    fw = np.zeros((NLON, 256), np.float32)
    fw[:, :KCOL] = lon_f
    iv = np.zeros((9, 2, 256, 256), np.float32)
    for n in range(9):
        low = min(256 * n // 360, 4)
        for s in range(2):
            for col in range(256):
                q = 256 * n + col - 360 * (low + s)
                if 0 <= q < 360:
                    iv[n, s, :KCOL, col] = lon_i[:, q]
    lat, chan = chunk_index()
    lf = np.zeros((16, NLAT, CHUNK), np.float32)
    for t in range(16):
        lf[t] = lat_f[:, 6 * t + np.maximum(lat, 0)] * (lat >= 0)
    lf = lf.reshape(NZ, 2, NLAT, CHUNK).transpose(0, 2, 1, 3).reshape(NZ, NLAT, 2 * CHUNK)
    spread = (chan[None, :] == np.arange(VARS)[:, None]).astype(np.float32)
    spread = np.concatenate([spread, spread], axis=1)
    return fw.astype(BF), iv.reshape(9, 512, 256).astype(BF), lf.astype(BF), lat_i, spread.astype(BF)


def dot(a, b):
    return jnp.dot(a, b, preferred_element_type=F32)


def forecast_kernel(nm, x_ref, fw_ref, iv_hbm, lf_hbm, li_ref, sp_ref, gain_ref, lift_ref, w1_ref, w2_ref, ro_ref,
                    count_ref, cell_ref, op_ref, val_ref, err_ref,
                    ft_ref, stats_ref,
                    spec, wmat, acc, bk, fs, field_ref, cp, lx, lt, w1t, w2t, rot, gt, turn, stage, xk, iv_ref, lf_ref, tab, part, got, mid, midg, fin,
                    ag_s, ag_r, ax_s, ax_r, rs_s, rs_r):
    m, t = lax.axis_index("member"), lax.axis_index("tile")
    nt = 2 * NZ
    z, core = t // 2, lax.rem(t, 2)

    def zat(d):
        return lax.rem(z + d + NZ, NZ)

    def member_peer(i):
        return (lax.rem(m + i, nm), t)

    def tile_peer(i):
        return (m, lax.rem(t + i, nt))

    right, left, sib = (m, zat(1) * 2 + core), (m, zat(-1) * 2 + core), (m, z * 2 + 1 - core)
    tables = [pltpu.make_async_copy(lf_hbm, lf_ref, tab.at[0]), pltpu.make_async_copy(iv_hbm, iv_ref, tab.at[1])]
    for cc in tables:
        cc.start()
    bar = pltpu.get_barrier_semaphore()
    for i in range(1, nt):
        pl.semaphore_signal(bar, inc=1, device_id=tile_peer(i), device_id_type=MESH)
    for i in range(1, nm):
        pl.semaphore_signal(bar, inc=1, device_id=member_peer(i), device_id_type=MESH)

    low64 = lax.broadcasted_iota(jnp.int32, (VARS, 128), 1) < 64
    low64e = lax.broadcasted_iota(jnp.int32, (EMB, 128), 1) < 64

    def half_turn(v):
        return pltpu.roll(v, 64, 1)

    state = [jnp.transpose(x_ref[:, p].astype(F32), (1, 0, 2)) for p in range(ROWS)]

    def spectra(pieces):
        tails = {i: [] for i in pieces}
        for p in range(ROWS):
            def both(e):
                v = dot(state[p][e].astype(BF), fw_ref[...])
                return v[:, :128], v[:, 128:]

            for i in pieces:
                if i == 0:
                    (a0, b0), (a1, _) = both(0), both(1)
                    v = [a0, jnp.where(low64, b0, half_turn(a1))]
                elif i == 1:
                    (a1, b1), (a2, _) = both(1), both(2)
                    v = [jnp.where(low64, half_turn(a1), half_turn(b1)), a2]
                else:
                    (_, b2), (a3, b3) = both(2), both(3)
                    a3 = half_turn(a3)
                    v = [jnp.where(low64, b2, a3), jnp.where(low64, a3, half_turn(b3))]
                v = jnp.concatenate(v, axis=1)
                spec[i, t, 64 * p:64 * p + 64] = v[:64].astype(BF)
                tails[i].append(v[64:VARS])
        for i in pieces:
            tails[i].append(jnp.zeros((10, 256), F32))
            spec[i, t, 384:CHUNK] = jnp.concatenate(tails[i], axis=0).astype(BF)

    def flatten():
        for e in range(4):
            v = jnp.concatenate([state[p][e] for p in range(ROWS)] + [jnp.zeros((VARS, CELLS - ROWS * NLON), F32)], axis=1)
            xk[e] = jnp.concatenate([v, jnp.zeros((CPAD - VARS, CELLS), F32)], axis=0).astype(BF)

    sent = []

    def copy(q, dz, other, h, sem, dev):
        rows = pl.ds(0, CHUNK) if h is None else pl.ds(h * (CHUNK // 2), CHUNK // 2)
        ref = spec.at[q, zat(dz) * 2 + (1 - core if other else core), rows]
        return pltpu.make_async_remote_copy(
            src_ref=ref, dst_ref=ref, send_sem=ag_s.at[q, sem], recv_sem=ag_r.at[q, sem],
            device_id=dev, device_id_type=MESH)

    def go(c):
        c.start()
        sent.append(c)

    def own(q):
        go(copy(q, 0, False, None, 0, right))
        go(copy(q, 0, False, None, 4, left))
        go(copy(q, 0, False, None, 8, sib))

    def step(q, d):
        for sign, base, h, dev in ((-1, 0, 0, right), (1, 4, 1, left)):
            copy(q, sign * d, False, h if d == 4 else None, base + d - 1, dev).wait_recv()
            if d < 4:
                go(copy(q, sign * d, False, h if d == 3 else None, base + d, dev))
        for sign, base, h in ((-1, 8, 0), (1, 12, 1)):
            go(copy(q, sign * d, False, h if d == 4 else None, base + d, sib))

    def from_sib(q, d):
        if d == 0:
            copy(q, 0, True, None, 8, sib).wait_recv()
        elif d == 4:
            copy(q, 4, True, 0, 12, sib).wait_recv()
            copy(q, 4, True, 1, 16, sib).wait_recv()
        else:
            copy(q, d, True, None, 8 - d if d < 0 else 12 + d, sib).wait_recv()

    def weights(d):
        zz = zat(d)

        @pl.loop(0, ROWS)
        def _(p):
            g = (gt[...] * li_ref[pl.ds(ROWS * t + p, 1), :]).astype(BF)
            w = dot(g, lf_ref[zz]).astype(BF)
            wmat[zz, pl.ds(pl.multiple_of(p * EMB, EMB), EMB), :] = w * lx[...]

    def apply(i, d, e, first=False):
        za, zb = zat(d), zat(e)
        g = jnp.concatenate([spec[i, pl.ds(zz * 2, 2)].reshape(2 * CHUNK, 256) for zz in (za, zb)], axis=0)

        @pl.loop(0, 3)
        def _(b):
            rows = pl.ds(pl.multiple_of(b * 512, 512), 512)
            v = dot(jnp.concatenate([wmat[za, rows, :], wmat[zb, rows, :]], axis=1), g)
            acc[i, rows, :] = v if first else acc[i, rows, :] + v

    c0 = math.sqrt(2.0 / math.pi)

    def member(e):
        @pl.loop(0, ROWS)
        def _(p):
            rows = pl.ds(pl.multiple_of(p * EMB, EMB), EMB)
            if e == 0:
                a = acc[0, rows, :]
            elif e == 2:
                a = jnp.concatenate([acc[1, rows, 128:], acc[2, rows, :128]], axis=1)
            else:
                head = half_turn(acc[0, rows, 128:] if e == 1 else acc[2, rows, :128])
                rest = half_turn(acc[1, rows, :128] if e == 1 else acc[2, rows, 128:])
                a = jnp.concatenate([jnp.where(low64e, head, rest), rest], axis=1)
            bk[p] = a.astype(BF)

        @pl.loop(0, 3)
        def _(it):
            lanes = pl.ds(pl.multiple_of(it * 768, 768), 768)
            x = xk[e, :, lanes]
            parts = []
            for k in range(3):
                n = 3 * it + k
                low = jnp.minimum(256 * n // 360, 4)
                parts.append(dot(jnp.concatenate([bk[low], bk[low + 1]], axis=1), iv_ref[n]))
            mixed = (jnp.concatenate(parts, axis=1) + dot(lt[...], x)).astype(BF)
            u = dot(w1t[...], mixed).astype(BF)
            h = 0.5 * u
            u = h * jnp.tanh(u * (c0 + (c0 * 0.044715) * (u * u))) + h
            outer = (mixed.astype(F32) + dot(w2t[...], u)).astype(BF)
            fs[e, :, lanes] = (x.astype(F32) + dot(rot[...], outer)).astype(BF)
            for k in range(6):
                to = 6 * it - 1 + k

                @pl.when((to >= 0) & (to < nm) & (to != m))
                def _():
                    out_copy(e, to).start()

        field_ref[nm * e + m] = fs[e, :, pl.ds(pl.multiple_of(128 * m, 128), 256)]

    def out_copy(e, to):
        return pltpu.make_async_remote_copy(
            src_ref=fs.at[e, :, pl.ds(pl.multiple_of(128 * to, 128), 256)], dst_ref=field_ref.at[nm * e + m],
            send_sem=ax_s.at[e, to], recv_sem=ax_r.at[e, m], device_id=(to, t), device_id_type=MESH)

    def in_copy(e, src):
        return pltpu.make_async_remote_copy(
            src_ref=fs.at[e, :, pl.ds(0, 256)], dst_ref=field_ref.at[nm * e + src],
            send_sem=ax_s.at[e, src], recv_sem=ax_r.at[e, src], device_id=(src, t), device_id_type=MESH)

    spectra((0,))
    pl.semaphore_wait(bar, nt + nm - 2)
    own(0)
    spectra((1,))
    own(1)
    spectra((2,))
    lv = jnp.concatenate([lift_ref[...].astype(F32), jnp.zeros((CPAD - VARS, EMB), F32)], axis=0).T.astype(BF)
    lt[...] = lv
    lx[...] = dot(lv[:, :VARS], sp_ref[...]).astype(BF)
    gt[...] = gain_ref[...].T
    tables[0].wait()
    weights(1)
    weights(-1)
    weights(2)
    weights(-2)
    step(0, 1)
    weights(3)
    step(1, 1)
    flatten()
    tables[1].wait()
    weights(-3)
    weights(0)
    from_sib(0, 1)
    from_sib(0, -1)
    apply(0, 1, -1, True)
    step(0, 2)
    own(2)
    weights(4)
    from_sib(1, 1)
    from_sib(1, -1)
    apply(1, 1, -1, True)
    step(1, 2)
    from_sib(0, 2)
    from_sib(0, -2)
    apply(0, 2, -2)
    step(0, 3)
    from_sib(1, 2)
    from_sib(1, -2)
    apply(1, 2, -2)
    step(2, 1)
    w1t[...] = w1_ref[...].astype(F32).T.astype(BF)
    w2t[...] = w2_ref[...].astype(F32).T.astype(BF)
    rot[...] = jnp.concatenate([ro_ref[...].astype(F32), jnp.zeros((CPAD - VARS, EMB), F32)], axis=0).astype(BF)
    step(1, 3)
    from_sib(0, 3)
    from_sib(0, -3)
    apply(0, 3, -3)
    step(0, 4)
    from_sib(1, 3)
    from_sib(1, -3)
    apply(1, 3, -3)
    step(1, 4)
    from_sib(0, 0)
    from_sib(0, 4)
    apply(0, 0, 4)
    step(2, 2)
    member(0)
    from_sib(2, 1)
    from_sib(2, -1)
    apply(2, 1, -1, True)
    step(2, 3)
    from_sib(1, 0)
    from_sib(1, 4)
    apply(1, 0, 4)
    from_sib(2, 2)
    from_sib(2, -2)
    apply(2, 2, -2)
    member(1)
    step(2, 4)
    from_sib(2, 3)
    from_sib(2, -3)
    apply(2, 3, -3)
    from_sib(2, 0)
    from_sib(2, 4)
    apply(2, 0, 4)
    member(2)
    member(3)

    cells = cell_ref[...] + 7 * m
    pick = (lax.broadcasted_iota(jnp.int32, (256, 128), 0) == cells).astype(BF)
    nt_dims = (((1,), (1,)), ((), ()))
    op = jnp.concatenate([op_ref[...].reshape(VARS, 128), jnp.zeros((CPAD - VARS, 128), F32)], axis=0)

    def counterparts(e, src):
        f = nm * e + src
        v = dot(field_ref[f], pick) * op
        cp[pl.ds(f, 1), :] = jnp.sum(v, axis=0, keepdims=True)

    def turned(g):
        @pl.loop(0, 16)
        def _(k):
            turn[k, :, :CPAD] = field_ref[16 * g + k].astype(F32).T

        for hf in range(2):
            v = turn[8 * hf:8 * hf + 8, pl.ds(7 * m, NCELL), :]
            stage[:, 8 * hf:8 * hf + 8, :] = jnp.transpose(v, (1, 0, 2))
        ft_ref[:, 16 * g:16 * g + 16, :] = stage[...].astype(BF)

    def collect(e):
        for i in range(nm):
            src = lax.rem(m - i + nm, nm)
            if i:
                in_copy(e, src).wait_recv()
            counterparts(e, src)

    for e in range(3):
        collect(e)
        turned(e)
    for cc in sent:
        cc.wait_send()
    sent.clear()
    for e in range(4):
        for i in range(1, nm):
            out_copy(e, lax.rem(m + i, nm)).wait_send()
    collect(3)
    c = cp[...]
    n = c.shape[0]
    ybar = jnp.mean(c, axis=0, keepdims=True)
    spread = c - ybar
    live = lax.broadcasted_iota(jnp.int32, (1, 128), 1) < count_ref[...]
    weight = jnp.where(live, 1.0 / err_ref[...], 0.0)
    both = jnp.concatenate([spread, val_ref[...] - ybar, jnp.zeros((127 - n, 128), F32)], axis=0)
    gram = lax.dot_general(spread * weight, both, nt_dims, precision=HI, preferred_element_type=F32)
    per = n // nt
    for b in range(nt):
        part[b, :per] = gram[per * b:per * b + per]
        part[b, per:] = jnp.zeros((8 - per, 128), F32)

    def send(src, dst, phase, i, dev):
        cc = pltpu.make_async_remote_copy(
            src_ref=src, dst_ref=dst, send_sem=rs_s.at[phase, i], recv_sem=rs_r.at[phase, i],
            device_id=dev, device_id_type=MESH)
        go(cc)
        return cc

    one = [send(part.at[lax.rem(t + i, nt)], got.at[i], 0, i, tile_peer(i)) for i in range(1, nt)]
    turned(3)
    tot = part[t]
    for cc in one:
        cc.wait_recv()
    for i in range(1, nt):
        tot = tot + got[i]
    mid[...] = tot
    two = [send(mid, midg.at[m], 1, i, member_peer(i)) for i in range(1, nm)]
    midg[m] = tot
    for cc in two:
        cc.wait_recv()
    tot = midg[0]
    for i in range(1, nm):
        tot = tot + midg[i]
    stats_ref[t] = tot
    fin[...] = tot
    three = [send(fin, stats_ref.at[t], 2, i, tile_peer(i)) for i in range(1, nt)]
    for cc in three:
        cc.wait_recv()
    for cc in sent:
        cc.wait_send()


def forecast_call(args, nm, nt, n):
    vm = pl.BlockSpec(memory_space=pltpu.VMEM)
    dma = pltpu.SemaphoreType.DMA
    return pl.pallas_call(
        functools.partial(forecast_kernel, nm),
        out_shape=[jax.ShapeDtypeStruct((NCELL, n, 128), BF), jax.ShapeDtypeStruct((nt, 8, 128), F32)],
        in_specs=[pl.BlockSpec(memory_space=pl.ANY) if i in (2, 3) else vm for i in range(len(args))],
        out_specs=[vm, vm],
        scratch_shapes=[
            pltpu.VMEM((3, nt, CHUNK, 256), BF),
            pltpu.VMEM((NZ, ROWS * EMB, 2 * CHUNK), BF),
            pltpu.VMEM((3, ROWS * EMB, 256), F32),
            pltpu.VMEM((ROWS, EMB, 256), BF),
            pltpu.VMEM((4, CPAD, CELLS), BF),
            pltpu.VMEM((n, CPAD, 256), BF),
            pltpu.VMEM((n, 128), F32),
            pltpu.VMEM((EMB, 2 * CHUNK), BF),
            pltpu.VMEM((EMB, CPAD), BF),
            pltpu.VMEM((HID, EMB), BF),
            pltpu.VMEM((EMB, HID), BF),
            pltpu.VMEM((CPAD, EMB), BF),
            pltpu.VMEM((EMB, NLAT), F32),
            pltpu.VMEM((16, 256, 128), F32),
            pltpu.VMEM((NCELL, 16, 128), F32),
            pltpu.VMEM((4, CPAD, CELLS), BF),
            pltpu.VMEM((9, 512, 256), BF),
            pltpu.VMEM((NZ, NLAT, 2 * CHUNK), BF),
            dma((2,)),
            pltpu.VMEM((nt, 8, 128), F32),
            pltpu.VMEM((nt, 8, 128), F32),
            pltpu.VMEM((8, 128), F32),
            pltpu.VMEM((nm, 8, 128), F32),
            pltpu.VMEM((8, 128), F32),
            dma((3, 17)), dma((3, 17)), dma((4, 16)), dma((4, 16)), dma((3, 16)), dma((3, 16)),
        ],
        compiler_params=pltpu.CompilerParams(
            collective_id=0, has_side_effects=True, vmem_limit_bytes=62 * 2**20),
        name="forecast",
    )(*args)


def split(a):
    hi = a.astype(BF)
    rest = a - hi.astype(F32)
    mid = rest.astype(BF)
    return hi, mid, (rest - mid.astype(F32)).astype(BF)


def mix_of(stats, n):
    rw = lax.broadcasted_iota(jnp.int32, (n, 128), 0)
    cw = lax.broadcasted_iota(jnp.int32, (n, 128), 1)
    low = cw < n
    wide = jnp.where(low, stats / (n - 1.0) + (rw == cw).astype(F32), stats)
    eye = ((rw == cw) | (rw + n == cw)).astype(F32)
    system = jnp.where(low, wide, pltpu.roll(wide, n, 1))
    scale = jnp.sqrt(0.5 * jnp.sum(system * system))

    def left(parts):
        hi, mid, lo = (v.astype(F32) for v in parts)
        return jnp.concatenate(
            [parts[0], jnp.where(low, mid, hi).astype(BF), jnp.where(low, lo, mid).astype(BF)], axis=1)

    def right(parts):
        hi, mid, lo = parts
        return jnp.concatenate([hi, mid, hi, lo, hi, mid], axis=0)

    up, root = system / scale, eye
    done = 0
    for it in range(NS_ITERS):
        su, sr = split(up), split(root)
        shift = 1.5 * eye - 0.5 * dot(left(sr), right(su))
        ss = split(shift)
        up = dot(left(su), right(ss))
        root = dot(left(ss), right(sr))
        upto = min(n, -(-n * (it + 1) // NS_ITERS))
        for j in range(done, upto):
            r = wide[j:j + 1, :]
            r = r / wide[j:j + 1, j:j + 1]
            col = wide[:, j:j + 1] - (rw[:, :1] == j).astype(F32)
            wide = wide - col * r
        done = upto
    weight = wide[:, n:n + 1] / (n - 1.0)
    return root[:, :n] / jnp.sqrt(scale) + weight


def analysis_kernel(stats_ref, field_ref, out_ref, ft, sem):
    n = ft.shape[1]
    nt = stats_ref.shape[0]
    load = pltpu.make_async_copy(field_ref, ft, sem)
    load.start()
    stats = jnp.concatenate([stats_ref[b, :n // nt] for b in range(nt)], axis=0)
    mix = mix_of(stats, n)
    mix = (mix + (1.0 - jnp.sum(mix, axis=0, keepdims=True)) / n).T
    hi = mix.astype(BF)
    lo = (mix - hi.astype(F32)).astype(BF)
    rows = lax.broadcasted_iota(jnp.int32, (n, n), 0)
    cols = lax.broadcasted_iota(jnp.int32, (n, n), 1)
    order = (cols == (n // 4) * (rows & 3) + (rows >> 2)).astype(BF)
    both = dot(order, jnp.concatenate([hi, lo], axis=1)).astype(BF)
    load.wait()
    step = 9

    @pl.loop(0, NCELL // step)
    def _(i):
        f = jnp.concatenate([ft[i * step + k] for k in range(step)], axis=1)
        v = dot(both, jnp.concatenate([f, f], axis=0))
        for k in range(step):
            out_ref[i * step + k] = v[:, 128 * k:128 * k + VARS].astype(BF)


def analysis_call(stats, ft):
    vm = pl.BlockSpec(memory_space=pltpu.VMEM)
    n = ft.shape[1]
    return pl.pallas_call(
        analysis_kernel,
        out_shape=jax.ShapeDtypeStruct((NCELL, n, VARS), BF),
        in_specs=[vm, pl.BlockSpec(memory_space=pl.ANY)],
        out_specs=vm,
        scratch_shapes=[pltpu.VMEM((NCELL, n, 128), BF), pltpu.SemaphoreType.DMA],
        compiler_params=pltpu.CompilerParams(vmem_limit_bytes=60 * 2**20),
        name="analysis",
    )(stats, ft)


def shards(x, lift, gain, w1, w2, readout, obs_count, obs_cell, obs_op, obs_value, obs_error):
    mem, nvar, rows, nlon = x.shape
    nt, nm = lax.axis_size("tile"), lax.axis_size("member")
    tables = (jnp.asarray(a) for a in kernel_tables())
    args = (jnp.transpose(x, (1, 2, 0, 3)), *tables, gain.T, lift, w1, w2, readout.T,
            obs_count.reshape(1, 1), obs_cell, obs_op.transpose(2, 0, 1), obs_value, obs_error)
    ft, stats = forecast_call(args, nm, nt, mem * nm)
    return jnp.transpose(analysis_call(stats, ft), (2, 0, 1))


def solution(mesh):
    placed = (
        P("member", None, "tile", None),
        P(), P(), P(), P(), P(),
        P(("tile", "member")),
        P(("tile", "member"), None),
        P(("tile", "member"), None, None),
        P(("tile", "member"), None),
        P(("tile", "member"), None),
    )
    return jax.shard_map(
        shards, mesh=mesh, in_specs=placed, out_specs=P(None, ("tile", "member"), None), check_vma=False)
```

```python
import functools
import math

import jax
import jax.numpy as jnp
import numpy as np
from jax import lax
from jax.experimental import pallas as pl
from jax.experimental.pallas import tpu as pltpu
from jax.sharding import PartitionSpec as P

MMAX = 96
NS_ITERS = 24
BF = jnp.bfloat16
F32 = jnp.float32
HI = lax.Precision.HIGHEST
MESH = pl.DeviceIdType.MESH


def lon_tables(nlon, mmax):
    lon = np.arange(nlon, dtype=np.float64)
    wave = np.arange(mmax, dtype=np.float64)
    phase = np.mod(lon[:, None] * wave[None, :], float(nlon))
    angle = 2.0 * math.pi * phase / nlon
    forward = np.concatenate([np.cos(angle), -np.sin(angle)], axis=1)
    factor = np.where(wave == 0.0, 1.0, 2.0) / nlon
    inverse = np.concatenate([np.cos(angle) * factor, -np.sin(angle) * factor], axis=1).T
    return (forward.astype(np.float32).astype(BF), inverse.astype(np.float32).astype(BF))


def lat_tables(nlat):
    row = np.arange(nlat, dtype=np.float64)
    phase = np.mod((2.0 * row[:, None] + 1.0) * row[None, :], float(4 * nlat))
    basis = np.cos(math.pi * phase / (2.0 * nlat))
    factor = np.where(row == 0.0, 1.0, 2.0) / nlat
    forward = (basis * factor[None, :]).T
    return (forward.astype(np.float32).astype(BF), basis.astype(np.float32).astype(BF))


VARS, CPAD = 73, 80
ROWS, NLON, NLAT = 6, 360, 96
KCOL = 2 * MMAX
CHUNK = 448
CELLS = 2304
EMB, HID = 256, 512
NZ = 8
NCELL = 135


def chunk_index():
    lat = np.full(CHUNK, -1)
    chan = np.full(CHUNK, -1)
    for p in range(ROWS):
        lat[64 * p:64 * p + 64], chan[64 * p:64 * p + 64] = p, np.arange(64)
        at = 384 + 9 * p
        lat[at:at + 9], chan[at:at + 9] = p, np.arange(64, 73)
    return lat, chan


def kernel_tables():
    lon_f, lon_i = (np.asarray(a).astype(np.float32) for a in lon_tables(NLON, MMAX))
    lat_f, lat_i = (np.asarray(a).astype(np.float32) for a in lat_tables(NLAT))
    fw = np.zeros((NLON, 256), np.float32)
    fw[:, :KCOL] = lon_f
    iv = np.zeros((9, 2, 256, 256), np.float32)
    for n in range(9):
        low = min(256 * n // 360, 4)
        for s in range(2):
            for col in range(256):
                q = 256 * n + col - 360 * (low + s)
                if 0 <= q < 360:
                    iv[n, s, :KCOL, col] = lon_i[:, q]
    lat, chan = chunk_index()
    lf = np.zeros((16, NLAT, CHUNK), np.float32)
    for t in range(16):
        lf[t] = lat_f[:, 6 * t + np.maximum(lat, 0)] * (lat >= 0)
    lf = lf.reshape(NZ, 2, NLAT, CHUNK).transpose(0, 2, 1, 3).reshape(NZ, NLAT, 2 * CHUNK)
    spread = (chan[None, :] == np.arange(VARS)[:, None]).astype(np.float32)
    spread = np.concatenate([spread, spread], axis=1)
    return fw.astype(BF), iv.reshape(9, 512, 256).astype(BF), lf.astype(BF), lat_i, spread.astype(BF)


def dot(a, b):
    return jnp.dot(a, b, preferred_element_type=F32)


def forecast_kernel(nm, x_ref, fw_ref, iv_hbm, lf_hbm, li_ref, sp_ref, gain_ref, lift_ref, w1_ref, w2_ref, ro_ref,
                    count_ref, cell_ref, op_ref, val_ref, err_ref,
                    ft_ref, stats_ref,
                    spec, wmat, acc, bk, fs, field_ref, cp, lx, lt, w1t, w2t, rot, gt, turn, stage, xk, iv_ref, lf_ref, tab, part, got, mid, midg, fin,
                    ag_s, ag_r, ax_s, ax_r, rs_s, rs_r):
    m, t = lax.axis_index("member"), lax.axis_index("tile")
    nt = 2 * NZ
    z, core = t // 2, lax.rem(t, 2)

    def zat(d):
        return lax.rem(z + d + NZ, NZ)

    def member_peer(i):
        return (lax.rem(m + i, nm), t)

    def tile_peer(i):
        return (m, lax.rem(t + i, nt))

    right, left, sib = (m, zat(1) * 2 + core), (m, zat(-1) * 2 + core), (m, z * 2 + 1 - core)
    tables = [pltpu.make_async_copy(lf_hbm, lf_ref, tab.at[0]), pltpu.make_async_copy(iv_hbm, iv_ref, tab.at[1])]
    for cc in tables:
        cc.start()
    bar = pltpu.get_barrier_semaphore()
    for i in range(1, nt):
        pl.semaphore_signal(bar, inc=1, device_id=tile_peer(i), device_id_type=MESH)
    for i in range(1, nm):
        pl.semaphore_signal(bar, inc=1, device_id=member_peer(i), device_id_type=MESH)

    low64 = lax.broadcasted_iota(jnp.int32, (VARS, 128), 1) < 64
    low64e = lax.broadcasted_iota(jnp.int32, (EMB, 128), 1) < 64

    def half_turn(v):
        return pltpu.roll(v, 64, 1)

    state = [jnp.transpose(x_ref[:, p].astype(F32), (1, 0, 2)) for p in range(ROWS)]

    def spectra(pieces):
        tails = {i: [] for i in pieces}
        for p in range(ROWS):
            def both(e):
                v = dot(state[p][e].astype(BF), fw_ref[...])
                return v[:, :128], v[:, 128:]

            for i in pieces:
                if i == 0:
                    (a0, b0), (a1, _) = both(0), both(1)
                    v = [a0, jnp.where(low64, b0, half_turn(a1))]
                elif i == 1:
                    (a1, b1), (a2, _) = both(1), both(2)
                    v = [jnp.where(low64, half_turn(a1), half_turn(b1)), a2]
                else:
                    (_, b2), (a3, b3) = both(2), both(3)
                    a3 = half_turn(a3)
                    v = [jnp.where(low64, b2, a3), jnp.where(low64, a3, half_turn(b3))]
                v = jnp.concatenate(v, axis=1)
                spec[i, t, 64 * p:64 * p + 64] = v[:64].astype(BF)
                tails[i].append(v[64:VARS])
        for i in pieces:
            tails[i].append(jnp.zeros((10, 256), F32))
            spec[i, t, 384:CHUNK] = jnp.concatenate(tails[i], axis=0).astype(BF)

    def flatten():
        for e in range(4):
            v = jnp.concatenate([state[p][e] for p in range(ROWS)] + [jnp.zeros((VARS, CELLS - ROWS * NLON), F32)], axis=1)
            xk[e] = jnp.concatenate([v, jnp.zeros((CPAD - VARS, CELLS), F32)], axis=0).astype(BF)

    sent = []

    def copy(q, dz, other, h, sem, dev):
        rows = pl.ds(0, CHUNK) if h is None else pl.ds(h * (CHUNK // 2), CHUNK // 2)
        ref = spec.at[q, zat(dz) * 2 + (1 - core if other else core), rows]
        return pltpu.make_async_remote_copy(
            src_ref=ref, dst_ref=ref, send_sem=ag_s.at[q, sem], recv_sem=ag_r.at[q, sem],
            device_id=dev, device_id_type=MESH)

    def go(c):
        c.start()
        sent.append(c)

    def own(q):
        go(copy(q, 0, False, None, 0, right))
        go(copy(q, 0, False, None, 4, left))
        go(copy(q, 0, False, None, 8, sib))

    def step(q, d):
        for sign, base, h, dev in ((-1, 0, 0, right), (1, 4, 1, left)):
            copy(q, sign * d, False, h if d == 4 else None, base + d - 1, dev).wait_recv()
            if d < 4:
                go(copy(q, sign * d, False, h if d == 3 else None, base + d, dev))
        for sign, base, h in ((-1, 8, 0), (1, 12, 1)):
            go(copy(q, sign * d, False, h if d == 4 else None, base + d, sib))

    def from_sib(q, d):
        if d == 0:
            copy(q, 0, True, None, 8, sib).wait_recv()
        elif d == 4:
            copy(q, 4, True, 0, 12, sib).wait_recv()
            copy(q, 4, True, 1, 16, sib).wait_recv()
        else:
            copy(q, d, True, None, 8 - d if d < 0 else 12 + d, sib).wait_recv()

    def weights(d):
        zz = zat(d)

        @pl.loop(0, 2)
        def _(b):
            g = [(gt[...] * li_ref[pl.ds(ROWS * t + 3 * b + k, 1), :]).astype(BF) for k in range(3)]
            w = dot(jnp.concatenate(g, axis=0), lf_ref[zz]).astype(BF)
            for k in range(3):
                rows = pl.ds(pl.multiple_of((3 * b + k) * EMB, EMB), EMB)
                wmat[zz, rows, :] = w[EMB * k:EMB * k + EMB] * lx[...]

    def apply(i, d, e, first=False):
        za, zb = zat(d), zat(e)
        g = jnp.concatenate([spec[i, pl.ds(zz * 2, 2)].reshape(2 * CHUNK, 256) for zz in (za, zb)], axis=0)

        v = dot(jnp.concatenate([wmat[za], wmat[zb]], axis=1), g)
        acc[i] = v if first else acc[i] + v

    c0 = math.sqrt(2.0 / math.pi)

    def member(e):
        @pl.loop(0, ROWS)
        def _(p):
            rows = pl.ds(pl.multiple_of(p * EMB, EMB), EMB)
            if e == 0:
                a = acc[0, rows, :]
            elif e == 2:
                a = jnp.concatenate([acc[1, rows, 128:], acc[2, rows, :128]], axis=1)
            else:
                head = half_turn(acc[0, rows, 128:] if e == 1 else acc[2, rows, :128])
                rest = half_turn(acc[1, rows, :128] if e == 1 else acc[2, rows, 128:])
                a = jnp.concatenate([jnp.where(low64e, head, rest), rest], axis=1)
            bk[p] = a.astype(BF)

        @pl.loop(0, 3)
        def _(it):
            lanes = pl.ds(pl.multiple_of(it * 768, 768), 768)
            x = xk[e, :, lanes]
            parts = []
            for k in range(3):
                n = 3 * it + k
                low = jnp.minimum(256 * n // 360, 4)
                parts.append(dot(jnp.concatenate([bk[low], bk[low + 1]], axis=1), iv_ref[n]))
            mixed = (jnp.concatenate(parts, axis=1) + dot(lt[...], x)).astype(BF)
            u = dot(w1t[...], mixed).astype(BF)
            h = 0.5 * u
            u = h * jnp.tanh(u * (c0 + (c0 * 0.044715) * (u * u))) + h
            outer = (mixed.astype(F32) + dot(w2t[...], u)).astype(BF)
            fs[e, :, lanes] = (x.astype(F32) + dot(rot[...], outer)).astype(BF)
            for k in range(6):
                to = 6 * it - 1 + k

                @pl.when((to >= 0) & (to < nm) & (to != m))
                def _():
                    out_copy(e, to).start()

        field_ref[nm * e + m] = fs[e, :, pl.ds(pl.multiple_of(128 * m, 128), 256)]

    def out_copy(e, to):
        return pltpu.make_async_remote_copy(
            src_ref=fs.at[e, :, pl.ds(pl.multiple_of(128 * to, 128), 256)], dst_ref=field_ref.at[nm * e + m],
            send_sem=ax_s.at[e, to], recv_sem=ax_r.at[e, m], device_id=(to, t), device_id_type=MESH)

    def in_copy(e, src):
        return pltpu.make_async_remote_copy(
            src_ref=fs.at[e, :, pl.ds(0, 256)], dst_ref=field_ref.at[nm * e + src],
            send_sem=ax_s.at[e, src], recv_sem=ax_r.at[e, src], device_id=(src, t), device_id_type=MESH)

    spectra((0,))
    pl.semaphore_wait(bar, nt + nm - 2)
    own(0)
    spectra((1,))
    own(1)
    spectra((2,))
    lv = jnp.concatenate([lift_ref[...].astype(F32), jnp.zeros((CPAD - VARS, EMB), F32)], axis=0).T.astype(BF)
    lt[...] = lv
    lx[...] = dot(lv[:, :VARS], sp_ref[...]).astype(BF)
    gt[...] = gain_ref[...].T
    tables[0].wait()
    weights(1)
    weights(-1)
    weights(2)
    weights(-2)
    step(0, 1)
    weights(3)
    step(1, 1)
    flatten()
    tables[1].wait()
    weights(-3)
    weights(0)
    from_sib(0, 1)
    from_sib(0, -1)
    apply(0, 1, -1, True)
    step(0, 2)
    own(2)
    weights(4)
    from_sib(1, 1)
    from_sib(1, -1)
    apply(1, 1, -1, True)
    step(1, 2)
    from_sib(0, 2)
    from_sib(0, -2)
    apply(0, 2, -2)
    step(0, 3)
    from_sib(1, 2)
    from_sib(1, -2)
    apply(1, 2, -2)
    step(2, 1)
    w1t[...] = w1_ref[...].astype(F32).T.astype(BF)
    w2t[...] = w2_ref[...].astype(F32).T.astype(BF)
    rot[...] = jnp.concatenate([ro_ref[...].astype(F32), jnp.zeros((CPAD - VARS, EMB), F32)], axis=0).astype(BF)
    step(1, 3)
    from_sib(0, 3)
    from_sib(0, -3)
    apply(0, 3, -3)
    step(0, 4)
    from_sib(1, 3)
    from_sib(1, -3)
    apply(1, 3, -3)
    step(1, 4)
    from_sib(0, 0)
    from_sib(0, 4)
    apply(0, 0, 4)
    step(2, 2)
    member(0)
    from_sib(2, 1)
    from_sib(2, -1)
    apply(2, 1, -1, True)
    step(2, 3)
    from_sib(1, 0)
    from_sib(1, 4)
    apply(1, 0, 4)
    from_sib(2, 2)
    from_sib(2, -2)
    apply(2, 2, -2)
    member(1)
    step(2, 4)
    from_sib(2, 3)
    from_sib(2, -3)
    apply(2, 3, -3)
    from_sib(2, 0)
    from_sib(2, 4)
    apply(2, 0, 4)
    member(2)
    member(3)

    cells = cell_ref[...] + 7 * m
    pick = (lax.broadcasted_iota(jnp.int32, (256, 128), 0) == cells).astype(BF)
    nt_dims = (((1,), (1,)), ((), ()))
    op = jnp.concatenate([op_ref[...].reshape(VARS, 128), jnp.zeros((CPAD - VARS, 128), F32)], axis=0)

    def counterparts(e, src):
        f = nm * e + src
        v = dot(field_ref[f], pick) * op
        cp[pl.ds(f, 1), :] = jnp.sum(v, axis=0, keepdims=True)

    def turned(g):
        @pl.loop(0, 16)
        def _(k):
            turn[k, :, :CPAD] = field_ref[16 * g + k].astype(F32).T

        for hf in range(2):
            v = turn[8 * hf:8 * hf + 8, pl.ds(7 * m, NCELL), :]
            stage[:, 8 * hf:8 * hf + 8, :] = jnp.transpose(v, (1, 0, 2))
        ft_ref[:, 16 * g:16 * g + 16, :] = stage[...].astype(BF)

    def collect(e):
        for i in range(nm):
            src = lax.rem(m - i + nm, nm)
            if i:
                in_copy(e, src).wait_recv()
            counterparts(e, src)

    for e in range(3):
        collect(e)
        turned(e)
    for cc in sent:
        cc.wait_send()
    sent.clear()
    for e in range(4):
        for i in range(1, nm):
            out_copy(e, lax.rem(m + i, nm)).wait_send()
    collect(3)
    c = cp[...]
    n = c.shape[0]
    ybar = jnp.mean(c, axis=0, keepdims=True)
    spread = c - ybar
    live = lax.broadcasted_iota(jnp.int32, (1, 128), 1) < count_ref[...]
    weight = jnp.where(live, 1.0 / err_ref[...], 0.0)
    both = jnp.concatenate([spread, val_ref[...] - ybar, jnp.zeros((127 - n, 128), F32)], axis=0)
    gram = lax.dot_general(spread * weight, both, nt_dims, precision=HI, preferred_element_type=F32)
    per = n // nt
    for b in range(nt):
        part[b, :per] = gram[per * b:per * b + per]
        part[b, per:] = jnp.zeros((8 - per, 128), F32)

    def send(src, dst, phase, i, dev):
        cc = pltpu.make_async_remote_copy(
            src_ref=src, dst_ref=dst, send_sem=rs_s.at[phase, i], recv_sem=rs_r.at[phase, i],
            device_id=dev, device_id_type=MESH)
        go(cc)
        return cc

    one = [send(part.at[lax.rem(t + i, nt)], got.at[i], 0, i, tile_peer(i)) for i in range(1, nt)]
    turned(3)
    tot = part[t]
    for cc in one:
        cc.wait_recv()
    for i in range(1, nt):
        tot = tot + got[i]
    mid[...] = tot
    two = [send(mid, midg.at[m], 1, i, member_peer(i)) for i in range(1, nm)]
    midg[m] = tot
    for cc in two:
        cc.wait_recv()
    tot = midg[0]
    for i in range(1, nm):
        tot = tot + midg[i]
    stats_ref[t] = tot
    fin[...] = tot
    three = [send(fin, stats_ref.at[t], 2, i, tile_peer(i)) for i in range(1, nt)]
    for cc in three:
        cc.wait_recv()
    for cc in sent:
        cc.wait_send()


def forecast_call(args, nm, nt, n):
    vm = pl.BlockSpec(memory_space=pltpu.VMEM)
    dma = pltpu.SemaphoreType.DMA
    return pl.pallas_call(
        functools.partial(forecast_kernel, nm),
        out_shape=[jax.ShapeDtypeStruct((NCELL, n, 128), BF), jax.ShapeDtypeStruct((nt, 8, 128), F32)],
        in_specs=[pl.BlockSpec(memory_space=pl.ANY) if i in (2, 3) else vm for i in range(len(args))],
        out_specs=[vm, vm],
        scratch_shapes=[
            pltpu.VMEM((3, nt, CHUNK, 256), BF),
            pltpu.VMEM((NZ, ROWS * EMB, 2 * CHUNK), BF),
            pltpu.VMEM((3, ROWS * EMB, 256), F32),
            pltpu.VMEM((ROWS, EMB, 256), BF),
            pltpu.VMEM((4, CPAD, CELLS), BF),
            pltpu.VMEM((n, CPAD, 256), BF),
            pltpu.VMEM((n, 128), F32),
            pltpu.VMEM((EMB, 2 * CHUNK), BF),
            pltpu.VMEM((EMB, CPAD), BF),
            pltpu.VMEM((HID, EMB), BF),
            pltpu.VMEM((EMB, HID), BF),
            pltpu.VMEM((CPAD, EMB), BF),
            pltpu.VMEM((EMB, NLAT), F32),
            pltpu.VMEM((16, 256, 128), F32),
            pltpu.VMEM((NCELL, 16, 128), F32),
            pltpu.VMEM((4, CPAD, CELLS), BF),
            pltpu.VMEM((9, 512, 256), BF),
            pltpu.VMEM((NZ, NLAT, 2 * CHUNK), BF),
            dma((2,)),
            pltpu.VMEM((nt, 8, 128), F32),
            pltpu.VMEM((nt, 8, 128), F32),
            pltpu.VMEM((8, 128), F32),
            pltpu.VMEM((nm, 8, 128), F32),
            pltpu.VMEM((8, 128), F32),
            dma((3, 17)), dma((3, 17)), dma((4, 16)), dma((4, 16)), dma((3, 16)), dma((3, 16)),
        ],
        compiler_params=pltpu.CompilerParams(
            collective_id=0, has_side_effects=True, vmem_limit_bytes=62 * 2**20),
        name="forecast",
    )(*args)


def split(a):
    hi = a.astype(BF)
    rest = a - hi.astype(F32)
    mid = rest.astype(BF)
    return hi, mid, (rest - mid.astype(F32)).astype(BF)


def mix_of(stats, n):
    rw = lax.broadcasted_iota(jnp.int32, (n, 128), 0)
    cw = lax.broadcasted_iota(jnp.int32, (n, 128), 1)
    low = cw < n
    wide = jnp.where(low, stats / (n - 1.0) + (rw == cw).astype(F32), stats)
    eye = ((rw == cw) | (rw + n == cw)).astype(F32)
    system = jnp.where(low, wide, pltpu.roll(wide, n, 1))
    scale = jnp.sqrt(0.5 * jnp.sum(system * system))

    def left(parts):
        hi, mid, lo = (v.astype(F32) for v in parts)
        return jnp.concatenate(
            [parts[0], jnp.where(low, mid, hi).astype(BF), jnp.where(low, lo, mid).astype(BF)], axis=1)

    def right(parts):
        hi, mid, lo = parts
        return jnp.concatenate([hi, mid, hi, lo, hi, mid], axis=0)

    up, root = system / scale, eye
    done = 0
    for it in range(NS_ITERS):
        su, sr = split(up), split(root)
        shift = 1.5 * eye - 0.5 * dot(left(sr), right(su))
        ss = split(shift)
        up = dot(left(su), right(ss))
        root = dot(left(ss), right(sr))
        upto = min(n, -(-n * (it + 1) // NS_ITERS))
        for j in range(done, upto):
            r = wide[j:j + 1, :]
            r = r / wide[j:j + 1, j:j + 1]
            col = wide[:, j:j + 1] - (rw[:, :1] == j).astype(F32)
            wide = wide - col * r
        done = upto
    weight = wide[:, n:n + 1] / (n - 1.0)
    return root[:, :n] / jnp.sqrt(scale) + weight


def analysis_kernel(stats_ref, field_ref, out_ref, ft, sem):
    n = ft.shape[1]
    nt = stats_ref.shape[0]
    load = pltpu.make_async_copy(field_ref, ft, sem)
    load.start()
    stats = jnp.concatenate([stats_ref[b, :n // nt] for b in range(nt)], axis=0)
    mix = mix_of(stats, n)
    mix = (mix + (1.0 - jnp.sum(mix, axis=0, keepdims=True)) / n).T
    hi = mix.astype(BF)
    lo = (mix - hi.astype(F32)).astype(BF)
    rows = lax.broadcasted_iota(jnp.int32, (n, n), 0)
    cols = lax.broadcasted_iota(jnp.int32, (n, n), 1)
    order = (cols == (n // 4) * (rows & 3) + (rows >> 2)).astype(BF)
    both = dot(order, jnp.concatenate([hi, lo], axis=1)).astype(BF)
    load.wait()
    step = 9

    @pl.loop(0, NCELL // step)
    def _(i):
        f = jnp.concatenate([ft[i * step + k] for k in range(step)], axis=1)
        v = dot(both, jnp.concatenate([f, f], axis=0))
        for k in range(step):
            out_ref[i * step + k] = v[:, 128 * k:128 * k + VARS].astype(BF)


def analysis_call(stats, ft):
    vm = pl.BlockSpec(memory_space=pltpu.VMEM)
    n = ft.shape[1]
    return pl.pallas_call(
        analysis_kernel,
        out_shape=jax.ShapeDtypeStruct((NCELL, n, VARS), BF),
        in_specs=[vm, pl.BlockSpec(memory_space=pl.ANY)],
        out_specs=vm,
        scratch_shapes=[pltpu.VMEM((NCELL, n, 128), BF), pltpu.SemaphoreType.DMA],
        compiler_params=pltpu.CompilerParams(vmem_limit_bytes=60 * 2**20),
        name="analysis",
    )(stats, ft)


def shards(x, lift, gain, w1, w2, readout, obs_count, obs_cell, obs_op, obs_value, obs_error):
    mem, nvar, rows, nlon = x.shape
    nt, nm = lax.axis_size("tile"), lax.axis_size("member")
    tables = (jnp.asarray(a) for a in kernel_tables())
    args = (jnp.transpose(x, (1, 2, 0, 3)), *tables, gain.T, lift, w1, w2, readout.T,
            obs_count.reshape(1, 1), obs_cell, obs_op.transpose(2, 0, 1), obs_value, obs_error)
    ft, stats = forecast_call(args, nm, nt, mem * nm)
    return jnp.transpose(analysis_call(stats, ft), (2, 0, 1))


def solution(mesh):
    placed = (
        P("member", None, "tile", None),
        P(), P(), P(), P(), P(),
        P(("tile", "member")),
        P(("tile", "member"), None),
        P(("tile", "member"), None, None),
        P(("tile", "member"), None),
        P(("tile", "member"), None),
    )
    return jax.shard_map(
        shards, mesh=mesh, in_specs=placed, out_specs=P(None, ("tile", "member"), None), check_vma=False)
```
